512 devices in a mesh: space: 16 (over y, x), member: 32 (over z, core).
Axes of the slice: x: 4, y: 4, z: 16, core: 2. Of those that a mesh axis runs over, the one named last changes fastest.
Arguments:
- state: bfloat16 [256, 8192, 128], P('member', 'space'), may hold values from -6 to 6
- obs_prior: bfloat16 [256, 256, 128], P('member', 'space'), may hold values from -6 to 6
- obs_value: float32 [256, 128], P('space'), may hold values from -6 to 6
- obs_precision: float32 [256, 128], P('space'), may hold values from 0.25 to 4
- block_lists: int32 [2048, 16], P(('space', 'member')), may hold values from 0 to 47, as said below
- list_counts: int32 [2048], P(('space', 'member')), may hold values from 4 to 16, as said below
Outputs:
- analysis: bfloat16 [256, 8192, 128], P('member', 'space')
The draws below stay inside these ranges and needn't reach their ends.
Inputs may be any that keep to these rules, and one draw needn't show every extreme that they name: `block_lists`: each row names 16 different blocks. `list_counts`: some group uses all 16 entries.
All inputs are finite; a program needn't handle non-finite values.
Results may differ from the reference program's by a relative error of at most 0.0055.
Values may be sent and summed in bfloat16 or wider, within the bound.
A program may use at most 64 MiB of HBM per device.

```python
import math
import jax
import jax.numpy as jnp
from jax import lax

MEMBERS = 256
CELLS = 128
OBS_BLK = 128
OB_TILE = 16
NL = 16
NS_ITERS = 6
GRP_TILE = 128
GROUPS = 2048
BLOCKS = 8192
OBS_BLOCKS = 256


def draw_block_lists(key, part):
    key = jax.random.fold_in(key, 11)
    subkeys = jax.random.split(key, GROUPS)
    return jax.vmap(lambda sub: jax.random.permutation(sub, 3 * OB_TILE)[:NL])(subkeys).astype(jnp.int32)


def draw_list_counts(key, part):
    key = jax.random.fold_in(key, 23)
    first, second = jax.random.split(key)
    counts = jax.random.randint(first, (GROUPS,), max(1, NL // 4), NL + 1)
    target = jax.random.randint(second, (), 0, GROUPS)
    return counts.at[target].set(NL).astype(jnp.int32)


def levels(key, shape, pieces, low, largest):
    factor_of = 1.0
    for axis_at, parts in pieces:
        heights = jax.random.uniform(jax.random.fold_in(jax.random.fold_in(key, 6), axis_at), (parts,), jnp.float32, low / len(pieces), largest / len(pieces))
        factor_of = factor_of * jnp.repeat(jnp.exp(heights), shape[axis_at] // parts).reshape((-1,) + (1,) * (len(shape) - 1 - axis_at))
    return factor_of


def bell_draw(key, shape, spread, bound, pieces=(), kind=jnp.bfloat16):
    entries = spread * jax.random.normal(key, shape, jnp.float32)
    if pieces:
        entries = entries * levels(key, shape, pieces, -0.22, 0.18)
    return jnp.clip(entries, -bound, bound).astype(kind)


def setup_inputs(seed: int = 0) -> dict:
    streams_of = jax.random.split(jax.random.key(seed), 7)
    state = bell_draw(streams_of[0], (MEMBERS, BLOCKS, CELLS), 1.0, 6.0, ((0, 32), (1, 16)))
    obs_prior = bell_draw(streams_of[1], (MEMBERS, OBS_BLOCKS, OBS_BLK), 1.0, 6.0, ((0, 32), (1, 16)))
    obs_value = bell_draw(streams_of[2], (OBS_BLOCKS, OBS_BLK), 1.0, 6.0, ((0, 16),), jnp.float32)
    obs_precision = jnp.clip(jnp.exp(math.log(4.0) - 2.7725887 * jax.random.uniform(streams_of[3], (OBS_BLOCKS, OBS_BLK), jnp.float32) ** levels(streams_of[3], (OBS_BLOCKS, OBS_BLK), ((0, 16),), -0.2, 0.2)), 0.25, 4.0)
    block_lists = draw_block_lists(jax.random.fold_in(streams_of[6], 71), 0)
    list_counts = draw_list_counts(jax.random.fold_in(streams_of[6], 71), 0)
    return {"state": state, "obs_prior": obs_prior, "obs_value": obs_value, "obs_precision": obs_precision, "block_lists": block_lists, "list_counts": list_counts}


def newton_schulz(system):
    size = system.shape[0]
    identity = jnp.eye(size, dtype=jnp.float32)
    frob_norm = jnp.sqrt(jnp.sum(system * system))
    iterate = system / frob_norm
    inverse_half = identity
    for sweep in range(NS_ITERS):
        factor = 1.5 * identity - 0.5 * jnp.dot(inverse_half, iterate, precision=lax.Precision.HIGHEST)
        iterate = jnp.dot(iterate, factor, precision=lax.Precision.HIGHEST)
        inverse_half = jnp.dot(factor, inverse_half, precision=lax.Precision.HIGHEST)
    return (inverse_half, frob_norm)

def solve_weights(picked, precision_rows, innovation_rows):
    members = picked.shape[0]
    matrix = picked.reshape(members, -1)
    weight_flat = precision_rows.reshape(-1)
    scaled = (matrix.astype(jnp.float32) * weight_flat).astype(jnp.bfloat16)
    product = lax.dot_general(matrix, scaled, (((1,), (1,)), ((), ())), preferred_element_type=jnp.float32)
    system = (members - 1.0) * jnp.eye(members, dtype=jnp.float32) + product
    weighted_innov = (weight_flat * innovation_rows.reshape(-1)).astype(jnp.bfloat16)
    forcing = jnp.dot(matrix, weighted_innov, preferred_element_type=jnp.float32)
    inverse_half, frob_norm = newton_schulz(system)
    inverse_full = jnp.dot(inverse_half, inverse_half, precision=lax.Precision.HIGHEST) / frob_norm
    weight_mean = jnp.dot(inverse_full, forcing, precision=lax.Precision.HIGHEST)
    return jnp.sqrt(members - 1.0) * inverse_half / jnp.sqrt(frob_norm) + weight_mean[:, None]

def apply_weights(xblock, weights):
    members = xblock.shape[0]
    matrix = xblock.reshape(members, -1).astype(jnp.float32)
    average = lax.optimization_barrier(jnp.mean(matrix, axis=0))
    departure = matrix - average
    updated = average + lax.dot_general(weights, departure, (((0,), (0,)), ((), ())), precision=lax.Precision.HIGHEST)
    return updated.astype(jnp.bfloat16).reshape(xblock.shape)

def reference(state, obs_prior, obs_value, obs_precision, block_lists, list_counts):
    prior32 = obs_prior.astype(jnp.float32)
    prior_mean = lax.optimization_barrier(jnp.mean(prior32, axis=0))
    anomaly = (prior32 - prior_mean).astype(jnp.bfloat16)
    innovation = obs_value - prior_mean
    anomaly_pad = jnp.pad(anomaly, ((0, 0), (OB_TILE, OB_TILE), (0, 0)))
    innov_pad = jnp.pad(innovation, ((OB_TILE, OB_TILE), (0, 0)))
    prec_pad = jnp.pad(obs_precision, ((OB_TILE, OB_TILE), (0, 0)))

    def solve(group):
        tile = group // GRP_TILE
        chosen = (tile * OB_TILE + block_lists[group]).astype(jnp.int32)
        picked = jnp.take(anomaly_pad, chosen, axis=1)
        active = (jnp.arange(NL, dtype=jnp.int32) < list_counts[group]).astype(jnp.float32)
        precision_rows = jnp.take(prec_pad, chosen, axis=0) * active[:, None]
        innovation_rows = jnp.take(innov_pad, chosen, axis=0)
        weights = solve_weights(picked, precision_rows, innovation_rows)
        xblock = lax.dynamic_slice_in_dim(state, (group * 4).astype(jnp.int32), 4, 1)
        return apply_weights(xblock, weights)
    result = lax.map(solve, jnp.arange(GROUPS, dtype=jnp.int32))
    return jnp.transpose(result, (1, 0, 2, 3)).reshape(MEMBERS, BLOCKS, CELLS)
```

```python
import math

import jax
import jax.numpy as jnp
from jax import lax
from jax.experimental import pallas as pl
from jax.experimental.pallas import tpu as pltpu
from jax.sharding import PartitionSpec as P

MESH = pl.DeviceIdType.MESH
BF, F32 = jnp.bfloat16, jnp.float32
NS_ITERS = 6
NG = 4
MEM = 256
NZ = 16
NSP = 16


def split(x):
    high = x.astype(BF)
    return high, (x - high.astype(F32)).astype(BF)


def dot(a, b):
    return lax.dot_general(a, b, (((1,), (0,)), ((), ())), preferred_element_type=F32)


def dot3(a, b):
    (ah, al), (bh, bl) = a, b
    return dot(jnp.concatenate([ah, al, ah], 1), jnp.concatenate([bh, bh, bl], 0))


def eye():
    rows = lax.broadcasted_iota(jnp.int32, (MEM, MEM), 0)
    return (rows == lax.broadcasted_iota(jnp.int32, (MEM, MEM), 1)).astype(F32)


def loop(low, high, body):
    def step(i, carry):
        body(i)
        return carry

    lax.fori_loop(low, high, step, 0)


def anomalies(s, raw, vp, stage, anom, prec, inno):
    for tile in range(3):
        def add(slot, total):
            return total + jnp.sum(raw[tile, slot].astype(F32), axis=0)

        mean = lax.fori_loop(0, 32, add, jnp.zeros((16, 128), F32)) * (1.0 / MEM)
        live = jnp.float32(1.0)
        if tile == 0:
            live = jnp.where(s > 0, 1.0, 0.0).astype(F32)
        if tile == 2:
            live = jnp.where(s < NSP - 1, 1.0, 0.0).astype(F32)

        def centre(slot):
            rows = (raw[tile, slot].astype(F32) - mean[None]) * live
            stage[pl.ds(pl.multiple_of(slot * 128, 128), 128), :] = rows.reshape(128, 128)

        loop(0, 32, centre)

        def pick(b):
            anom[tile * 16 + b] = stage[pl.ds(b, MEM, stride=16), :].astype(BF)

        loop(0, 16, pick)
        innovation = (vp[tile, 0] - mean) * live
        precision = vp[tile, 1] * live
        for b in range(16):
            inno[tile * 16 + b] = innovation[b : b + 1]
            prec[tile * 16 + b] = precision[b : b + 1]


def systems(lists, counts, anom, prec, inno, t_ref, f_ref):
    def group(g):
        count = counts[g]
        total = jnp.zeros((MEM + 16, MEM), F32)
        for pair in range(8):
            ys, ss, ws = [], [], []
            for e in (2 * pair, 2 * pair + 1):
                b = lists[g, e]
                y = anom[b]
                r = prec[b] * jnp.where(e < count, 1.0, 0.0).astype(F32)
                ys.append(y)
                ss.append((y.astype(F32) * r).astype(BF))
                ws.append(jnp.broadcast_to((r * inno[b]).astype(BF), (16, 128)))
            left = jnp.concatenate([jnp.concatenate(ss, 1), jnp.concatenate(ws, 1)], 0)
            total = total + lax.dot_general(
                left, jnp.concatenate(ys, 1), (((1,), (1,)), ((), ())), preferred_element_type=F32
            )
        t_ref[g] = total[:MEM] + (MEM - 1.0) * eye()
        f_ref[g] = total[MEM:]

    loop(0, NG, group)


def weights(t_ref, f_ref, p_ref, z_ref, w_ref):
    def first(g):
        t = t_ref[g]
        norm = jnp.sqrt(jnp.sum(t * t, keepdims=True))
        iterate = t / norm
        factor = split(1.5 * eye() - 0.5 * iterate)
        z_ref[g, 0], z_ref[g, 1] = factor
        p_ref[g, 0], p_ref[g, 1] = split(dot3(split(iterate), factor))
        t_ref[g, 0:8, 0:128] = jnp.broadcast_to(norm, (8, 128))

    loop(0, NG, first)

    def sweep(step):
        g = lax.rem(step, NG)
        z = z_ref[g, 0], z_ref[g, 1]
        p = p_ref[g, 0], p_ref[g, 1]
        factor = split(1.5 * eye() - 0.5 * dot3(z, p))
        p_ref[g, 0], p_ref[g, 1] = split(dot3(p, factor))
        z_ref[g, 0], z_ref[g, 1] = split(dot3(factor, z))

    loop(0, (NS_ITERS - 1) * NG, sweep)

    def last(g):
        z = z_ref[g, 0], z_ref[g, 1]
        norm = t_ref[g, 0:1, 0:1]
        mean = dot3(split(dot3(split(f_ref[g]), z)), z)[0:1] / norm
        w = (z[0].astype(F32) + z[1].astype(F32)) * (math.sqrt(MEM - 1.0) / jnp.sqrt(norm)) + mean
        w = w + (1.0 - jnp.sum(w, axis=1, keepdims=True)) * (1.0 / MEM)
        w_ref[g, 0], w_ref[g, 1] = split(w)

    loop(0, NG, last)


def kernel(
    lists, counts, state, obs, value, precision, out,
    raw, vp, stage, anom, prec, inno, t_ref, f_ref, p_ref, z_ref, w_ref, cols, xb, stage2, outb,
    rps, rpr, rms, rmr, sbs, sbr, has, har, shs, shr, vps, vpr, s1, r1, s2, r2, own,
):
    s, me = lax.axis_index("space"), lax.axis_index("member")
    z, c = me // 2, me % 2
    zp, zm = ((z + 1) % NZ) * 2 + c, ((z + NZ - 1) % NZ) * 2 + c
    sibling = z * 2 + 1 - c
    up, down = (s + 1) % NSP, (s + NSP - 1) % NSP

    barrier = pltpu.get_barrier_semaphore()
    for peer in (up, down):
        pl.semaphore_signal(barrier, inc=1, device_id=(peer, me), device_id_type=MESH)

    def greet(d):
        pl.semaphore_signal(barrier, inc=1, device_id=(s, (me + d) % 32), device_id_type=MESH)

    loop(1, 32, greet)
    pl.semaphore_wait(barrier, 33)

    def rcopy(src, dst, ss, rs, device):
        return pltpu.make_async_remote_copy(
            src_ref=src, dst_ref=dst, send_sem=ss, recv_sem=rs, device_id=device, device_id_type=MESH
        )

    def ring_up(t):
        return rcopy(raw.at[1, 2 * ((16 - t) % 16)], raw.at[1, 2 * (15 - t)], rps.at[t], rpr.at[t], (s, zp))

    def ring_down(t):
        return rcopy(raw.at[1, 2 * t], raw.at[1, 2 * (t + 1)], rms.at[t], rmr.at[t], (s, zm))

    def across(u):
        return rcopy(raw.at[1, 2 * u], raw.at[1, 2 * u + 1], sbs.at[u], sbr.at[u], (s, sibling))

    def halo(side, u):
        dst = raw.at[2 * side, 2 * u]
        return rcopy(raw.at[1, 2 * u], dst, has.at[side, u], har.at[side, u], ((up, down)[side], me))

    def halo_across(side, u):
        tile = 2 * side
        return rcopy(
            raw.at[tile, 2 * u], raw.at[tile, 2 * u + 1], shs.at[side, u], shr.at[side, u], (s, sibling)
        )

    def rim(side):
        return rcopy(vp.at[1], vp.at[2 * side], vps.at[side], vpr.at[side], ((up, down)[side], me))

    def far(j):
        return (8 + ((j + 1) // 2) * (2 * ((j + 1) % 2) - 1)) % 16

    def place(u, p):
        core = c if p == 0 else 1 - c
        return 2 * ((z + u) % NZ) + core

    def rows_of(member):
        return pl.ds(pl.multiple_of(member * 16, 16), 16)

    def send_state(u, p):
        target = place(u, p)
        slot = 2 * ((16 - u) % 16) + p
        return rcopy(
            state.at[:, rows_of(target), :], cols.at[slot], s1.at[2 * u + p], r1.at[slot], (s, target)
        )

    def send_result(u, p):
        target = place(u, p)
        slot = 2 * ((16 - u) % 16) + p
        return rcopy(
            outb.at[2 * u + p], out.at[:, rows_of(me), :], s2.at[2 * u + p], r2.at[slot], (s, target)
        )

    def spread(u):
        across(u).start()
        halo(0, u).start()
        halo(1, u).start()

    def relay(u):
        for side in range(2):
            halo(side, u).wait_recv()
            halo_across(side, u).start()

    own_in = pltpu.make_async_copy(state.at[:, rows_of(me), :], cols.at[0], own.at[0])
    own_in.start()
    raw[1, 0] = obs[...]
    vp[1, 0] = value[...]
    vp[1, 1] = precision[...]
    ring_up(0).start()
    ring_down(0).start()
    spread(0)
    rim(0).start()
    rim(1).start()

    def scatter(j):
        u = far(j)
        send_state(u, 0).start()
        send_state(u, 1).start()

    scatter(0)
    scatter(1)

    def step(t):
        ring_up(t - 1).wait_recv()
        ring_up(t).start()
        ring_down(t - 1).wait_recv()

        @pl.when(t < 7)
        def _():
            ring_down(t).start()

        spread(16 - t)
        spread(t)

        @pl.when(t > 1)
        def _():
            relay(17 - t)
            relay(t - 1)

        scatter(2 * t)

        @pl.when(t < 7)
        def _():
            scatter(2 * t + 1)

    loop(1, 8, step)
    send_state(0, 1).start()
    ring_up(7).wait_recv()
    spread(8)
    relay(0)
    relay(9)
    relay(7)
    relay(8)

    def landed(u):
        across(u).wait_recv()
        halo_across(0, u).wait_recv()
        halo_across(1, u).wait_recv()

    loop(0, 16, landed)
    rim(0).wait_recv()
    rim(1).wait_recv()

    anomalies(s, raw, vp, stage, anom, prec, inno)
    systems(lists, counts, anom, prec, inno, t_ref, f_ref)
    weights(t_ref, f_ref, p_ref, z_ref, w_ref)

    def unpack(slot):
        rows = cols[slot].astype(F32).reshape(128, 128)
        stage[pl.ds(pl.multiple_of(slot * 128, 128), 128), :] = rows

    own_in.wait()
    unpack(0)

    def arrive(slot):
        rcopy(
            state.at[:, pl.ds(0, 16), :], cols.at[slot], s1.at[slot], r1.at[slot], (s, sibling)
        ).wait_recv()
        unpack(slot)

    loop(1, 32, arrive)
    for g in range(NG):
        for r in range(4):
            xb[g, :, r * 128 : (r + 1) * 128] = stage[pl.ds(4 * g + r, MEM, stride=16), :].astype(BF)

    def apply(part):
        far_of = [far(4 * part + i) for i in range(4)]
        for g in range(NG):
            left = [
                w_ref[g, h, pl.ds(pl.multiple_of(u * 16, 16), 16), :] for h in range(2) for u in far_of
            ]
            both = dot(jnp.concatenate(left, 0), xb[g])
            done = both[:64] + both[64:]
            for r in range(4):
                stage2[pl.ds(4 * g + r, 64, stride=16), :] = done[:, r * 128 : (r + 1) * 128]
        for i, u in enumerate(far_of):
            for p in range(2):
                rows = stage2[pl.ds((2 * i + p) * 128, 128), :]
                outb[2 * u + p] = rows.reshape(8, 16, 128).astype(BF)
                if i == 3 and p == 0:

                    @pl.when(part < 3)
                    def _():
                        send_result(u, p).start()
                else:
                    send_result(u, p).start()

    loop(0, 4, apply)
    own_out = pltpu.make_async_copy(outb.at[0], out.at[:, rows_of(me), :], own.at[1])
    own_out.start()

    def settle(slot):
        rcopy(
            outb.at[slot], out.at[:, pl.ds(0, 16), :], s2.at[slot], r2.at[slot], (s, sibling)
        ).wait()
        rcopy(
            state.at[:, pl.ds(0, 16), :], cols.at[slot], s1.at[slot], r1.at[slot], (s, sibling)
        ).wait_send()

    loop(1, 32, settle)
    own_out.wait()

    def sent(t):
        ring_up(t).wait_send()

        @pl.when(t < 7)
        def _():
            ring_down(t).wait_send()

    loop(0, 8, sent)

    def sent_wide(u):
        across(u).wait_send()
        for side in range(2):
            halo(side, u).wait_send()
            halo_across(side, u).wait_send()

    loop(0, 16, sent_wide)
    rim(0).wait_send()
    rim(1).wait_send()


def per_device(state, obs_prior, obs_value, obs_precision, block_lists, list_counts):
    vmem = pl.BlockSpec(memory_space=pltpu.VMEM)
    smem = pl.BlockSpec(memory_space=pltpu.SMEM)
    anywhere = pl.BlockSpec(memory_space=pl.ANY)
    dma = pltpu.SemaphoreType.DMA
    return pl.pallas_call(
        kernel,
        out_shape=jax.ShapeDtypeStruct(state.shape, state.dtype),
        in_specs=[smem, smem, anywhere, vmem, vmem, vmem],
        out_specs=anywhere,
        scratch_shapes=[
            pltpu.VMEM((3, 32, 8, 16, 128), BF),
            pltpu.VMEM((3, 2, 16, 128), F32),
            pltpu.VMEM((4096, 128), F32),
            pltpu.VMEM((48, MEM, 128), BF),
            pltpu.VMEM((48, 1, 128), F32),
            pltpu.VMEM((48, 1, 128), F32),
            pltpu.VMEM((NG, MEM, MEM), F32),
            pltpu.VMEM((NG, 16, MEM), F32),
            pltpu.VMEM((NG, 2, MEM, MEM), BF),
            pltpu.VMEM((NG, 2, MEM, MEM), BF),
            pltpu.VMEM((NG, 2, MEM, MEM), BF),
            pltpu.VMEM((32, 8, 16, 128), BF),
            pltpu.VMEM((NG, MEM, 512), BF),
            pltpu.VMEM((1024, 128), F32),
            pltpu.VMEM((32, 8, 16, 128), BF),
            dma((8,)), dma((8,)), dma((7,)), dma((7,)), dma((16,)), dma((16,)),
            dma((2, 16)), dma((2, 16)), dma((2, 16)), dma((2, 16)), dma((2,)), dma((2,)),
            dma((32,)), dma((32,)), dma((32,)), dma((32,)), dma((2,)),
        ],
        compiler_params=pltpu.CompilerParams(
            collective_id=0, has_side_effects=True, vmem_limit_bytes=48 << 20
        ),
        name="analysis",
    )(block_lists, list_counts, state, obs_prior, obs_value, obs_precision)


def solution(mesh):
    in_specs = (
        P("member", "space", None),
        P("member", "space", None),
        P("space", None),
        P("space", None),
        P(("space", "member"), None),
        P(("space", "member")),
    )
    out_specs = P("member", "space", None)
    return jax.shard_map(
        per_device, mesh=mesh, in_specs=in_specs, out_specs=out_specs, check_vma=False
    )
```

```python
import math

import jax
import jax.numpy as jnp
from jax import lax
from jax.experimental import pallas as pl
from jax.experimental.pallas import tpu as pltpu
from jax.sharding import PartitionSpec as P

MESH = pl.DeviceIdType.MESH
BF, F32 = jnp.bfloat16, jnp.float32
NS_ITERS = 6
NG = 4
MEM = 256
NZ = 16
NSP = 16


def split(x):
    high = x.astype(BF)
    return high, (x - high.astype(F32)).astype(BF)


def dot(a, b):
    return lax.dot_general(a, b, (((1,), (0,)), ((), ())), preferred_element_type=F32)


def dot3(a, b):
    (ah, al), (bh, bl) = a, b
    return dot(jnp.concatenate([ah, al, ah], 1), jnp.concatenate([bh, bh, bl], 0))


def eye():
    rows = lax.broadcasted_iota(jnp.int32, (MEM, MEM), 0)
    return (rows == lax.broadcasted_iota(jnp.int32, (MEM, MEM), 1)).astype(F32)


def loop(low, high, body):
    def step(i, carry):
        body(i)
        return carry

    lax.fori_loop(low, high, step, 0)


def anomalies(s, raw, vp, stage, anom, prec, inno):
    for tile in range(3):
        def add(slot, total):
            return total + jnp.sum(raw[tile, slot].astype(F32), axis=0)

        mean = lax.fori_loop(0, 32, add, jnp.zeros((16, 128), F32)) * (1.0 / MEM)
        live = jnp.float32(1.0)
        if tile == 0:
            live = jnp.where(s > 0, 1.0, 0.0).astype(F32)
        if tile == 2:
            live = jnp.where(s < NSP - 1, 1.0, 0.0).astype(F32)

        def centre(slot):
            rows = (raw[tile, slot].astype(F32) - mean[None]) * live
            stage[pl.ds(pl.multiple_of(slot * 128, 128), 128), :] = rows.reshape(128, 128)

        loop(0, 32, centre)

        def pick(b):
            anom[tile * 16 + b] = stage[pl.ds(b, MEM, stride=16), :].astype(BF)

        loop(0, 16, pick)
        innovation = (vp[tile, 0] - mean) * live
        precision = vp[tile, 1] * live
        for b in range(16):
            inno[tile * 16 + b] = innovation[b : b + 1]
            prec[tile * 16 + b] = precision[b : b + 1]


def systems(lists, counts, anom, prec, inno, t_ref, f_ref):
    def group(g):
        count = counts[g]
        total = jnp.zeros((MEM + 16, MEM), F32)
        for pair in range(8):
            ys, ss, ws = [], [], []
            for e in (2 * pair, 2 * pair + 1):
                b = lists[g, e]
                y = anom[b]
                r = prec[b] * jnp.where(e < count, 1.0, 0.0).astype(F32)
                ys.append(y)
                ss.append((y.astype(F32) * r).astype(BF))
                ws.append(jnp.broadcast_to((r * inno[b]).astype(BF), (16, 128)))
            left = jnp.concatenate([jnp.concatenate(ss, 1), jnp.concatenate(ws, 1)], 0)
            total = total + lax.dot_general(
                left, jnp.concatenate(ys, 1), (((1,), (1,)), ((), ())), preferred_element_type=F32
            )
        t_ref[g] = total[:MEM] + (MEM - 1.0) * eye()
        f_ref[g] = total[MEM:]

    loop(0, NG, group)


def weights(t_ref, f_ref, p_ref, z_ref, w_ref):
    def first(g):
        t = t_ref[g]
        norm = jnp.sqrt(jnp.sum(t * t, keepdims=True))
        iterate = t / norm
        factor = split(1.5 * eye() - 0.5 * iterate)
        z_ref[g, 0], z_ref[g, 1] = factor
        p_ref[g, 0], p_ref[g, 1] = split(dot3(split(iterate), factor))
        t_ref[g, 0:8, 0:128] = jnp.broadcast_to(norm, (8, 128))

    loop(0, NG, first)

    def sweep(step):
        g = lax.rem(step, NG)
        z = z_ref[g, 0], z_ref[g, 1]
        p = p_ref[g, 0], p_ref[g, 1]
        factor = split(1.5 * eye() - 0.5 * dot3(z, p))
        p_ref[g, 0], p_ref[g, 1] = split(dot3(p, factor))
        z_ref[g, 0], z_ref[g, 1] = split(dot3(factor, z))

    loop(0, (NS_ITERS - 1) * NG, sweep)

    def last(g):
        z = z_ref[g, 0], z_ref[g, 1]
        norm = t_ref[g, 0:1, 0:1]
        mean = dot3(split(dot3(split(f_ref[g]), z)), z)[0:1] / norm
        w = (z[0].astype(F32) + z[1].astype(F32)) * (math.sqrt(MEM - 1.0) / jnp.sqrt(norm)) + mean
        w = w + (1.0 - jnp.sum(w, axis=1, keepdims=True)) * (1.0 / MEM)
        w_ref[g, 0], w_ref[g, 1] = split(w)

    loop(0, NG, last)


def kernel(
    lists_in, counts_in, state, obs, value, precision, out,
    lists, counts, raw, vp, stage, anom, prec, inno, t_ref, f_ref, p_ref, z_ref, w_ref, cols, xb, stage2, outb,
    r1s, r1r, r2s, r2r, sbs, sbr, has, har, shs, shr, vps, vpr, s1, r1, s2, r2, own,
):
    s, me = lax.axis_index("space"), lax.axis_index("member")
    z, c = me // 2, me % 2
    sibling = z * 2 + 1 - c
    up, down = (s + 1) % NSP, (s + NSP - 1) % NSP

    loads = [
        pltpu.make_async_copy(src, dst, own.at[i])
        for i, (src, dst) in enumerate((
            (state.at[:, pl.ds(pl.multiple_of(me * 16, 16), 16), :], cols.at[0]),
            (lists_in, lists),
            (counts_in, counts),
            (obs, raw.at[1, 0]),
            (value, vp.at[1, 0]),
            (precision, vp.at[1, 1]),
        ))
    ]
    for load in loads:
        load.start()

    barrier = pltpu.get_barrier_semaphore()
    for peer in (up, down):
        pl.semaphore_signal(barrier, inc=1, device_id=(peer, me), device_id_type=MESH)

    def greet(d):
        pl.semaphore_signal(barrier, inc=1, device_id=(s, (me + d) % 32), device_id_type=MESH)

    loop(1, 32, greet)
    pl.semaphore_wait(barrier, 33)

    def rcopy(src, dst, ss, rs, device):
        return pltpu.make_async_remote_copy(
            src_ref=src, dst_ref=dst, send_sem=ss, recv_sem=rs, device_id=device, device_id_type=MESH
        )

    def hop(side, far, k):
        d = 2 * k + 1 + far
        now, then = ((16 - 2 * k) % 16, 16 - d) if side == 0 else (2 * k, d)
        sems = (r1s, r1r) if far == 0 else (r2s, r2r)
        dz = (1 + far) if side == 0 else NZ - 1 - far
        peer = ((z + dz) % NZ) * 2 + c
        return rcopy(
            raw.at[1, 2 * now], raw.at[1, 2 * then], sems[0].at[side, k], sems[1].at[side, k], (s, peer)
        )

    def across(u):
        return rcopy(raw.at[1, 2 * u], raw.at[1, 2 * u + 1], sbs.at[u], sbr.at[u], (s, sibling))

    def halo(side, u):
        dst = raw.at[2 * side, 2 * u]
        return rcopy(raw.at[1, 2 * u], dst, has.at[side, u], har.at[side, u], ((up, down)[side], me))

    def halo_across(side, u):
        tile = 2 * side
        return rcopy(
            raw.at[tile, 2 * u], raw.at[tile, 2 * u + 1], shs.at[side, u], shr.at[side, u], (s, sibling)
        )

    def rim(side):
        return rcopy(vp.at[1], vp.at[2 * side], vps.at[side], vpr.at[side], ((up, down)[side], me))

    def far(j):
        return (8 + ((j + 1) // 2) * (2 * ((j + 1) % 2) - 1)) % 16

    def place(u, p):
        core = c if p == 0 else 1 - c
        return 2 * ((z + u) % NZ) + core

    def rows_of(member):
        return pl.ds(pl.multiple_of(member * 16, 16), 16)

    def send_state(u, p):
        target = place(u, p)
        slot = 2 * ((16 - u) % 16) + p
        return rcopy(
            state.at[:, rows_of(target), :], cols.at[slot], s1.at[2 * u + p], r1.at[slot], (s, target)
        )

    def send_result(u, p):
        target = place(u, p)
        slot = 2 * ((16 - u) % 16) + p
        return rcopy(
            outb.at[2 * u + p], out.at[:, rows_of(me), :], s2.at[2 * u + p], r2.at[slot], (s, target)
        )

    def spread(u):
        across(u).start()
        halo(0, u).start()
        halo(1, u).start()

    def relay(u):
        for side in range(2):
            halo(side, u).wait_recv()
            halo_across(side, u).start()

    def scatter(u):
        send_state(u, 0).start()
        send_state(u, 1).start()

    for load in loads[3:]:
        load.wait()
    for side in range(2):
        hop(side, 1, 0).start()
    for side in range(2):
        hop(side, 0, 0).start()
    spread(0)
    rim(0).start()
    rim(1).start()
    for k in range(1, 4):
        for side in range(2):
            hop(side, 1, k - 1).wait_recv()
            if k < 3 or side == 0:
                hop(side, 1, k).start()
        for side in range(2):
            hop(side, 0, k).start()
        spread(16 - 2 * k)
        spread(2 * k)
        for side in range(2):
            hop(side, 0, k - 1).wait_recv()
            spread((17 - 2 * k, 2 * k - 1)[side])
        if k == 1:
            relay(0)
        else:
            for d in (2 * k - 3, 2 * k - 2):
                relay(16 - d)
                relay(d)
        scatter(k)
        scatter(16 - k)
    for side in range(2):
        hop(side, 0, 3).wait_recv()
        spread((9, 7)[side])
    hop(0, 1, 3).wait_recv()
    spread(8)
    scatter(4)
    scatter(12)
    send_state(0, 1).start()
    for d in (5, 6, 7, 8):
        relay(16 - d)
        if d < 8:
            relay(d)
    loop(0, 7, lambda j: scatter(far(j)))

    def landed(u):
        across(u).wait_recv()
        halo_across(0, u).wait_recv()
        halo_across(1, u).wait_recv()

    loop(0, 16, landed)
    rim(0).wait_recv()
    rim(1).wait_recv()

    loads[1].wait()
    loads[2].wait()
    anomalies(s, raw, vp, stage, anom, prec, inno)
    systems(lists, counts, anom, prec, inno, t_ref, f_ref)
    weights(t_ref, f_ref, p_ref, z_ref, w_ref)

    def unpack(slot):
        rows = cols[slot].astype(F32).reshape(128, 128)
        stage[pl.ds(pl.multiple_of(slot * 128, 128), 128), :] = rows

    loads[0].wait()
    unpack(0)

    def arrive(slot):
        rcopy(
            state.at[:, pl.ds(0, 16), :], cols.at[slot], s1.at[slot], r1.at[slot], (s, sibling)
        ).wait_recv()
        unpack(slot)

    loop(1, 32, arrive)
    for g in range(NG):
        for r in range(4):
            xb[g, :, r * 128 : (r + 1) * 128] = stage[pl.ds(4 * g + r, MEM, stride=16), :].astype(BF)

    def apply(part):
        far_of = [far(4 * part + i) for i in range(4)]
        for g in range(NG):
            left = [
                w_ref[g, h, pl.ds(pl.multiple_of(u * 16, 16), 16), :] for h in range(2) for u in far_of
            ]
            both = dot(jnp.concatenate(left, 0), xb[g])
            done = both[:64] + both[64:]
            for r in range(4):
                stage2[pl.ds(4 * g + r, 64, stride=16), :] = done[:, r * 128 : (r + 1) * 128]
        for i, u in enumerate(far_of):
            for p in range(2):
                rows = stage2[pl.ds((2 * i + p) * 128, 128), :]
                outb[2 * u + p] = rows.reshape(8, 16, 128).astype(BF)
                if i == 3 and p == 0:

                    @pl.when(part < 3)
                    def _():
                        send_result(u, p).start()
                else:
                    send_result(u, p).start()

    loop(0, 4, apply)
    own_out = pltpu.make_async_copy(outb.at[0], out.at[:, rows_of(me), :], own.at[6])
    own_out.start()

    def settle(slot):
        rcopy(
            outb.at[slot], out.at[:, pl.ds(0, 16), :], s2.at[slot], r2.at[slot], (s, sibling)
        ).wait()
        rcopy(
            state.at[:, pl.ds(0, 16), :], cols.at[slot], s1.at[slot], r1.at[slot], (s, sibling)
        ).wait_send()

    loop(1, 32, settle)
    own_out.wait()

    for side in range(2):
        for k in range(4):
            hop(side, 0, k).wait_send()
            if side == 0 or k < 3:
                hop(side, 1, k).wait_send()

    def sent_wide(u):
        across(u).wait_send()
        for side in range(2):
            halo(side, u).wait_send()
            halo_across(side, u).wait_send()

    loop(0, 16, sent_wide)
    rim(0).wait_send()
    rim(1).wait_send()


def per_device(state, obs_prior, obs_value, obs_precision, block_lists, list_counts):
    anywhere = pl.BlockSpec(memory_space=pl.ANY)
    dma = pltpu.SemaphoreType.DMA
    return pl.pallas_call(
        kernel,
        out_shape=jax.ShapeDtypeStruct(state.shape, state.dtype),
        in_specs=[anywhere] * 6,
        out_specs=anywhere,
        scratch_shapes=[
            pltpu.SMEM((NG, 16), jnp.int32),
            pltpu.SMEM((NG,), jnp.int32),
            pltpu.VMEM((3, 32, 8, 16, 128), BF),
            pltpu.VMEM((3, 2, 16, 128), F32),
            pltpu.VMEM((4096, 128), F32),
            pltpu.VMEM((48, MEM, 128), BF),
            pltpu.VMEM((48, 1, 128), F32),
            pltpu.VMEM((48, 1, 128), F32),
            pltpu.VMEM((NG, MEM, MEM), F32),
            pltpu.VMEM((NG, 16, MEM), F32),
            pltpu.VMEM((NG, 2, MEM, MEM), BF),
            pltpu.VMEM((NG, 2, MEM, MEM), BF),
            pltpu.VMEM((NG, 2, MEM, MEM), BF),
            pltpu.VMEM((32, 8, 16, 128), BF),
            pltpu.VMEM((NG, MEM, 512), BF),
            pltpu.VMEM((1024, 128), F32),
            pltpu.VMEM((32, 8, 16, 128), BF),
            dma((2, 4)), dma((2, 4)), dma((2, 4)), dma((2, 4)), dma((16,)), dma((16,)),
            dma((2, 16)), dma((2, 16)), dma((2, 16)), dma((2, 16)), dma((2,)), dma((2,)),
            dma((32,)), dma((32,)), dma((32,)), dma((32,)), dma((7,)),
        ],
        compiler_params=pltpu.CompilerParams(
            collective_id=0, has_side_effects=True, vmem_limit_bytes=62 << 20
        ),
        name="analysis",
    )(block_lists, list_counts, state, obs_prior, obs_value, obs_precision)


def solution(mesh):
    in_specs = (
        P("member", "space", None),
        P("member", "space", None),
        P("space", None),
        P("space", None),
        P(("space", "member"), None),
        P(("space", "member")),
    )
    out_specs = P("member", "space", None)
    return jax.shard_map(
        per_device, mesh=mesh, in_specs=in_specs, out_specs=out_specs, check_vma=False
    )
```

```python
import math

import jax
import jax.numpy as jnp
from jax import lax
from jax.experimental import pallas as pl
from jax.experimental.pallas import tpu as pltpu
from jax.sharding import PartitionSpec as P

MESH = pl.DeviceIdType.MESH
BF, F32 = jnp.bfloat16, jnp.float32
NS_ITERS = 6
NG = 4
MEM = 256
NZ = 16
NSP = 16
SCHED = (
    ((1, 0), (2, 0)),
    ((1, 1), (2, 1)),
    ((3, 0), (4, 0)),
    ((3, 1), (4, 1), (5, 0)),
    ((6, 0), (5, 1)),
    ((8, 0), (8, 1), (7, 0), (7, 1), (6, 1)),
)


def split(x):
    high = x.astype(BF)
    return high, (x - high.astype(F32)).astype(BF)


def dot(a, b):
    return lax.dot_general(a, b, (((1,), (0,)), ((), ())), preferred_element_type=F32)


def dot3(a, b):
    (ah, al), (bh, bl) = a, b
    return dot(jnp.concatenate([ah, al, ah], 1), jnp.concatenate([bh, bh, bl], 0))


def eye():
    rows = lax.broadcasted_iota(jnp.int32, (MEM, MEM), 0)
    return (rows == lax.broadcasted_iota(jnp.int32, (MEM, MEM), 1)).astype(F32)


def loop(low, high, body):
    def step(i, carry):
        body(i)
        return carry

    lax.fori_loop(low, high, step, 0)


def anomalies(s, raw, vp, stage, anom, prec, inno):
    for tile in range(3):
        def add(slot, total):
            return total + jnp.sum(raw[tile, slot].astype(F32), axis=0)

        mean = lax.fori_loop(0, 32, add, jnp.zeros((16, 128), F32)) * (1.0 / MEM)
        live = jnp.float32(1.0)
        if tile == 0:
            live = jnp.where(s > 0, 1.0, 0.0).astype(F32)
        if tile == 2:
            live = jnp.where(s < NSP - 1, 1.0, 0.0).astype(F32)

        def centre(slot):
            rows = (raw[tile, slot].astype(F32) - mean[None]) * live
            stage[pl.ds(pl.multiple_of(slot * 128, 128), 128), :] = rows.reshape(128, 128)

        loop(0, 32, centre)

        def pick(b):
            anom[tile * 16 + b] = stage[pl.ds(b, MEM, stride=16), :].astype(BF)

        loop(0, 16, pick)
        innovation = (vp[tile, 0] - mean) * live
        precision = vp[tile, 1] * live
        for b in range(16):
            inno[tile * 16 + b] = innovation[b : b + 1]
            prec[tile * 16 + b] = precision[b : b + 1]


def systems(lists, counts, anom, prec, inno, t_ref, f_ref):
    def group(g):
        count = counts[g]
        total = jnp.zeros((MEM + 16, MEM), F32)
        for pair in range(8):
            ys, ss, ws = [], [], []
            for e in (2 * pair, 2 * pair + 1):
                b = lists[g, e]
                y = anom[b]
                r = prec[b] * jnp.where(e < count, 1.0, 0.0).astype(F32)
                ys.append(y)
                ss.append((y.astype(F32) * r).astype(BF))
                ws.append(jnp.broadcast_to((r * inno[b]).astype(BF), (16, 128)))
            left = jnp.concatenate([jnp.concatenate(ss, 1), jnp.concatenate(ws, 1)], 0)
            total = total + lax.dot_general(
                left, jnp.concatenate(ys, 1), (((1,), (1,)), ((), ())), preferred_element_type=F32
            )
        t_ref[g] = total[:MEM] + (MEM - 1.0) * eye()
        f_ref[g] = total[MEM:]

    loop(0, NG, group)


def weights(t_ref, f_ref, p_ref, z_ref, w_ref):
    def first(g):
        t = t_ref[g]
        norm = jnp.sqrt(jnp.sum(t * t, keepdims=True))
        iterate = t / norm
        factor = split(1.5 * eye() - 0.5 * iterate)
        z_ref[g, 0], z_ref[g, 1] = factor
        p_ref[g, 0], p_ref[g, 1] = split(dot3(split(iterate), factor))
        t_ref[g, 0:8, 0:128] = jnp.broadcast_to(norm, (8, 128))

    loop(0, NG, first)

    def sweep(step):
        g = lax.rem(step, NG)
        z = z_ref[g, 0], z_ref[g, 1]
        p = p_ref[g, 0], p_ref[g, 1]
        factor = split(1.5 * eye() - 0.5 * dot3(z, p))
        p_ref[g, 0], p_ref[g, 1] = split(dot3(p, factor))
        z_ref[g, 0], z_ref[g, 1] = split(dot3(factor, z))

    loop(0, (NS_ITERS - 1) * NG, sweep)

    def last(g):
        z = z_ref[g, 0], z_ref[g, 1]
        norm = t_ref[g, 0:1, 0:1]
        mean = dot3(split(dot3(split(f_ref[g]), z)), z)[0:1] / norm
        w = (z[0].astype(F32) + z[1].astype(F32)) * (math.sqrt(MEM - 1.0) / jnp.sqrt(norm)) + mean
        w = w + (1.0 - jnp.sum(w, axis=1, keepdims=True)) * (1.0 / MEM)
        w_ref[g, 0], w_ref[g, 1] = split(w)

    loop(0, NG, last)


def kernel(
    lists_in, counts_in, state, obs, value, precision, out,
    lists, counts, raw, vp, stage, anom, prec, inno, t_ref, f_ref, p_ref, z_ref, w_ref, cols, xb, stage2, outb,
    r1s, r1r, r2s, r2r, sbs, sbr, has, har, shs, shr, vps, vpr, s1, r1, s2, r2, own,
):
    s, me = lax.axis_index("space"), lax.axis_index("member")
    z, c = me // 2, me % 2
    sibling = z * 2 + 1 - c
    up, down = (s + 1) % NSP, (s + NSP - 1) % NSP

    loads = [
        pltpu.make_async_copy(src, dst, own.at[i])
        for i, (src, dst) in enumerate((
            (state.at[:, pl.ds(pl.multiple_of(me * 16, 16), 16), :], cols.at[0]),
            (lists_in, lists),
            (counts_in, counts),
            (obs, raw.at[1, 0]),
            (value, vp.at[1, 0]),
            (precision, vp.at[1, 1]),
        ))
    ]
    for load in loads:
        load.start()

    barrier = pltpu.get_barrier_semaphore()
    near = [(s, ((z + d) % NZ) * 2 + c) for d in (1, 2, NZ - 2, NZ - 1)]
    near += [(s, sibling), (up, me), (down, me)]
    for peer in near:
        pl.semaphore_signal(barrier, inc=1, device_id=peer, device_id_type=MESH)
    pl.semaphore_wait(barrier, len(near))

    def rcopy(src, dst, ss, rs, device):
        return pltpu.make_async_remote_copy(
            src_ref=src, dst_ref=dst, send_sem=ss, recv_sem=rs, device_id=device, device_id_type=MESH
        )

    def hop(side, far, k):
        d = 2 * k + 1 + far
        now, then = ((16 - 2 * k) % 16, 16 - d) if side == 0 else (2 * k, d)
        sems = (r1s, r1r) if far == 0 else (r2s, r2r)
        dz = (1 + far) if side == 0 else NZ - 1 - far
        peer = ((z + dz) % NZ) * 2 + c
        return rcopy(
            raw.at[1, 2 * now], raw.at[1, 2 * then], sems[0].at[side, k], sems[1].at[side, k], (s, peer)
        )

    def across(u):
        return rcopy(raw.at[1, 2 * u], raw.at[1, 2 * u + 1], sbs.at[u], sbr.at[u], (s, sibling))

    def halo(side, u):
        dst = raw.at[2 * side, 2 * u]
        return rcopy(raw.at[1, 2 * u], dst, has.at[side, u], har.at[side, u], ((up, down)[side], me))

    def halo_across(side, u):
        tile = 2 * side
        return rcopy(
            raw.at[tile, 2 * u], raw.at[tile, 2 * u + 1], shs.at[side, u], shr.at[side, u], (s, sibling)
        )

    def rim(side):
        return rcopy(vp.at[1], vp.at[2 * side], vps.at[side], vpr.at[side], ((up, down)[side], me))

    def far(j):
        return (8 + ((j + 1) // 2) * (2 * ((j + 1) % 2) - 1)) % 16

    def place(u, p):
        core = c if p == 0 else 1 - c
        return 2 * ((z + u) % NZ) + core

    def rows_of(member):
        return pl.ds(pl.multiple_of(member * 16, 16), 16)

    def send_state(u, p):
        target = place(u, p)
        slot = 2 * ((16 - u) % 16) + p
        return rcopy(
            state.at[:, rows_of(target), :], cols.at[slot], s1.at[2 * u + p], r1.at[slot], (s, target)
        )

    def send_result(u, p):
        target = place(u, p)
        slot = 2 * ((16 - u) % 16) + p
        return rcopy(
            outb.at[2 * u + p], out.at[:, rows_of(me), :], s2.at[2 * u + p], r2.at[slot], (s, target)
        )

    def spread(u):
        across(u).start()
        halo(0, u).start()
        halo(1, u).start()

    def relay(u):
        for side in range(2):
            halo(side, u).wait_recv()
            halo_across(side, u).start()

    def scatter(d, p):
        if p == 1:
            across(d).wait_recv()
        send_state(d, p).start()
        if d < 8:
            if p == 1:
                across(16 - d).wait_recv()
            send_state(16 - d, p).start()

    def sched(i):
        for d, p in SCHED[i]:
            scatter(d, p)

    for load in loads[3:]:
        load.wait()
    for side in range(2):
        hop(side, 1, 0).start()
    for side in range(2):
        hop(side, 0, 0).start()
    spread(0)
    rim(0).start()
    rim(1).start()
    sched(0)
    for k in range(1, 4):
        for side in range(2):
            hop(side, 1, k - 1).wait_recv()
            if k < 3 or side == 0:
                hop(side, 1, k).start()
        for side in range(2):
            hop(side, 0, k).start()
        spread(16 - 2 * k)
        spread(2 * k)
        for side in range(2):
            hop(side, 0, k - 1).wait_recv()
            spread((17 - 2 * k, 2 * k - 1)[side])
        if k == 1:
            relay(0)
        else:
            for d in (2 * k - 3, 2 * k - 2):
                relay(16 - d)
                relay(d)
        sched(k)
    for side in range(2):
        hop(side, 0, 3).wait_recv()
        spread((9, 7)[side])
    hop(0, 1, 3).wait_recv()
    spread(8)
    sched(4)
    across(0).wait_recv()
    send_state(0, 1).start()
    for d in (5, 6, 7, 8):
        relay(16 - d)
        if d < 8:
            relay(d)
    sched(5)

    def landed(u):
        halo_across(0, u).wait_recv()
        halo_across(1, u).wait_recv()

    loop(0, 16, landed)
    rim(0).wait_recv()
    rim(1).wait_recv()

    loads[1].wait()
    loads[2].wait()
    anomalies(s, raw, vp, stage, anom, prec, inno)
    systems(lists, counts, anom, prec, inno, t_ref, f_ref)
    weights(t_ref, f_ref, p_ref, z_ref, w_ref)

    def unpack(slot):
        rows = cols[slot].astype(F32).reshape(128, 128)
        stage[pl.ds(pl.multiple_of(slot * 128, 128), 128), :] = rows

    loads[0].wait()
    unpack(0)

    def arrive(slot):
        rcopy(
            state.at[:, pl.ds(0, 16), :], cols.at[slot], s1.at[slot], r1.at[slot], (s, sibling)
        ).wait_recv()
        unpack(slot)

    loop(1, 32, arrive)
    for g in range(NG):
        for r in range(4):
            xb[g, :, r * 128 : (r + 1) * 128] = stage[pl.ds(4 * g + r, MEM, stride=16), :].astype(BF)

    def apply(part):
        far_of = [far(4 * part + i) for i in range(4)]
        for g in range(NG):
            left = [
                w_ref[g, h, pl.ds(pl.multiple_of(u * 16, 16), 16), :] for h in range(2) for u in far_of
            ]
            both = dot(jnp.concatenate(left, 0), xb[g])
            done = both[:64] + both[64:]
            for r in range(4):
                stage2[pl.ds(4 * g + r, 64, stride=16), :] = done[:, r * 128 : (r + 1) * 128]
        for i, u in enumerate(far_of):
            for p in range(2):
                rows = stage2[pl.ds((2 * i + p) * 128, 128), :]
                outb[2 * u + p] = rows.reshape(8, 16, 128).astype(BF)
                if i == 3 and p == 0:

                    @pl.when(part < 3)
                    def _():
                        send_result(u, p).start()
                else:
                    send_result(u, p).start()

    loop(0, 4, apply)
    own_out = pltpu.make_async_copy(outb.at[0], out.at[:, rows_of(me), :], own.at[6])
    own_out.start()

    def settle(slot):
        rcopy(
            outb.at[slot], out.at[:, pl.ds(0, 16), :], s2.at[slot], r2.at[slot], (s, sibling)
        ).wait()
        rcopy(
            state.at[:, pl.ds(0, 16), :], cols.at[slot], s1.at[slot], r1.at[slot], (s, sibling)
        ).wait_send()

    loop(1, 32, settle)
    own_out.wait()

    for side in range(2):
        for k in range(4):
            hop(side, 0, k).wait_send()
            if side == 0 or k < 3:
                hop(side, 1, k).wait_send()

    def sent_wide(u):
        across(u).wait_send()
        for side in range(2):
            halo(side, u).wait_send()
            halo_across(side, u).wait_send()

    loop(0, 16, sent_wide)
    rim(0).wait_send()
    rim(1).wait_send()


def per_device(state, obs_prior, obs_value, obs_precision, block_lists, list_counts):
    anywhere = pl.BlockSpec(memory_space=pl.ANY)
    dma = pltpu.SemaphoreType.DMA
    return pl.pallas_call(
        kernel,
        out_shape=jax.ShapeDtypeStruct(state.shape, state.dtype),
        in_specs=[anywhere] * 6,
        out_specs=anywhere,
        scratch_shapes=[
            pltpu.SMEM((NG, 16), jnp.int32),
            pltpu.SMEM((NG,), jnp.int32),
            pltpu.VMEM((3, 32, 8, 16, 128), BF),
            pltpu.VMEM((3, 2, 16, 128), F32),
            pltpu.VMEM((4096, 128), F32),
            pltpu.VMEM((48, MEM, 128), BF),
            pltpu.VMEM((48, 1, 128), F32),
            pltpu.VMEM((48, 1, 128), F32),
            pltpu.VMEM((NG, MEM, MEM), F32),
            pltpu.VMEM((NG, 16, MEM), F32),
            pltpu.VMEM((NG, 2, MEM, MEM), BF),
            pltpu.VMEM((NG, 2, MEM, MEM), BF),
            pltpu.VMEM((NG, 2, MEM, MEM), BF),
            pltpu.VMEM((32, 8, 16, 128), BF),
            pltpu.VMEM((NG, MEM, 512), BF),
            pltpu.VMEM((1024, 128), F32),
            pltpu.VMEM((32, 8, 16, 128), BF),
            dma((2, 4)), dma((2, 4)), dma((2, 4)), dma((2, 4)), dma((16,)), dma((16,)),
            dma((2, 16)), dma((2, 16)), dma((2, 16)), dma((2, 16)), dma((2,)), dma((2,)),
            dma((32,)), dma((32,)), dma((32,)), dma((32,)), dma((7,)),
        ],
        compiler_params=pltpu.CompilerParams(
            collective_id=0, has_side_effects=True, vmem_limit_bytes=62 << 20
        ),
        name="analysis",
    )(block_lists, list_counts, state, obs_prior, obs_value, obs_precision)


def solution(mesh):
    in_specs = (
        P("member", "space", None),
        P("member", "space", None),
        P("space", None),
        P("space", None),
        P(("space", "member"), None),
        P(("space", "member")),
    )
    out_specs = P("member", "space", None)
    return jax.shard_map(
        per_device, mesh=mesh, in_specs=in_specs, out_specs=out_specs, check_vma=False
    )
```

```python
import math

import jax
import jax.numpy as jnp
from jax import lax
from jax.experimental import pallas as pl
from jax.experimental.pallas import tpu as pltpu
from jax.sharding import PartitionSpec as P

MESH = pl.DeviceIdType.MESH
BF, F32 = jnp.bfloat16, jnp.float32
NS_ITERS = 6
NG = 4
MEM = 256
NZ = 16
NSP = 16
SCHED = (
    ((1, 0), (2, 0)),
    ((2, 1),),
    ((3, 0), (4, 0)),
    ((4, 1), (5, 0)),
    ((6, 0), (5, 1)),
    ((8, 0), (8, 1), (7, 0), (7, 1), (6, 1), (3, 1), (1, 1)),
)


def split(x):
    high = x.astype(BF)
    return high, (x - high.astype(F32)).astype(BF)


def dot(a, b):
    return lax.dot_general(a, b, (((1,), (0,)), ((), ())), preferred_element_type=F32)


def dot3(a, b):
    (ah, al), (bh, bl) = a, b
    return dot(jnp.concatenate([ah, al, ah], 1), jnp.concatenate([bh, bh, bl], 0))


def eye():
    rows = lax.broadcasted_iota(jnp.int32, (MEM, MEM), 0)
    return (rows == lax.broadcasted_iota(jnp.int32, (MEM, MEM), 1)).astype(F32)


def loop(low, high, body):
    def step(i, carry):
        body(i)
        return carry

    lax.fori_loop(low, high, step, 0)


def anomalies(tile, raw, vp, stage, anom, prec, inno):
    def add(slot, total):
        return total + jnp.sum(raw[tile, slot].astype(F32), axis=0)

    mean = lax.fori_loop(0, 32, add, jnp.zeros((16, 128), F32)) * (1.0 / MEM)

    def centre(slot):
        rows = raw[tile, slot].astype(F32) - mean[None]
        stage[pl.ds(pl.multiple_of(slot * 128, 128), 128), :] = rows.reshape(128, 128)

    loop(0, 32, centre)

    def pick(b):
        anom[tile * 16 + b] = stage[pl.ds(b, MEM, stride=16), :].astype(BF)

    loop(0, 16, pick)
    innovation = vp[tile, 0] - mean
    precision = vp[tile, 1]
    for b in range(16):
        inno[tile * 16 + b] = innovation[b : b + 1]
        prec[tile * 16 + b] = precision[b : b + 1]


def no_tile(tile, anom, prec, inno):
    def clear(b):
        anom[tile * 16 + b] = jnp.zeros((MEM, 128), BF)
        inno[tile * 16 + b] = jnp.zeros((1, 128), F32)
        prec[tile * 16 + b] = jnp.zeros((1, 128), F32)

    loop(0, 16, clear)


def systems(lists, counts, anom, prec, inno, t_ref, f_ref):
    def group(g):
        count = counts[g]
        total = jnp.zeros((MEM + 16, MEM), F32)
        for pair in range(8):
            ys, ss, ws = [], [], []
            for e in (2 * pair, 2 * pair + 1):
                b = lists[g, e]
                y = anom[b]
                r = prec[b] * jnp.where(e < count, 1.0, 0.0).astype(F32)
                ys.append(y)
                ss.append((y.astype(F32) * r).astype(BF))
                ws.append(jnp.broadcast_to((r * inno[b]).astype(BF), (16, 128)))
            left = jnp.concatenate([jnp.concatenate(ss, 1), jnp.concatenate(ws, 1)], 0)
            total = total + lax.dot_general(
                left, jnp.concatenate(ys, 1), (((1,), (1,)), ((), ())), preferred_element_type=F32
            )
        t_ref[g] = total[:MEM] + (MEM - 1.0) * eye()
        f_ref[g] = total[MEM:]

    loop(0, NG, group)


def weights(t_ref, f_ref, p_ref, z_ref, w_ref):
    def first(g):
        t = t_ref[g]
        norm = jnp.sqrt(jnp.sum(t * t, keepdims=True))
        iterate = t / norm
        factor = split(1.5 * eye() - 0.5 * iterate)
        z_ref[g, 0], z_ref[g, 1] = factor
        p_ref[g, 0], p_ref[g, 1] = split(dot3(split(iterate), factor))
        t_ref[g, 0:8, 0:128] = jnp.broadcast_to(norm, (8, 128))

    loop(0, NG, first)

    def sweep(step):
        g = lax.rem(step, NG)
        z = z_ref[g, 0], z_ref[g, 1]
        p = p_ref[g, 0], p_ref[g, 1]
        factor = split(1.5 * eye() - 0.5 * dot3(z, p))
        p_ref[g, 0], p_ref[g, 1] = split(dot3(p, factor))
        z_ref[g, 0], z_ref[g, 1] = split(dot3(factor, z))

    loop(0, (NS_ITERS - 1) * NG, sweep)

    def last(g):
        z = z_ref[g, 0], z_ref[g, 1]
        norm = t_ref[g, 0:1, 0:1]
        mean = dot3(split(dot3(split(f_ref[g]), z)), z)[0:1] / norm
        w = (z[0].astype(F32) + z[1].astype(F32)) * (math.sqrt(MEM - 1.0) / jnp.sqrt(norm)) + mean
        w = w + (1.0 - jnp.sum(w, axis=1, keepdims=True)) * (1.0 / MEM)
        w_ref[g, 0], w_ref[g, 1] = split(w)

    loop(0, NG, last)


def kernel(
    lists_in, counts_in, state, obs, value, precision, out,
    lists, counts, raw, vp, stage, anom, prec, inno, t_ref, f_ref, p_ref, z_ref, w_ref, cols, xb, stage2, outb,
    r1s, r1r, r2s, r2r, sbs, sbr, has, har, shs, shr, vps, vpr, s1, r1, s2, r2, own,
):
    s, me = lax.axis_index("space"), lax.axis_index("member")
    z, c = me // 2, me % 2
    sibling = z * 2 + 1 - c
    up, down = (s + 1) % NSP, (s + NSP - 1) % NSP
    has_up, has_down = s < NSP - 1, s > 0

    def toward(side, body):
        pl.when((has_up, has_down)[side])(body)

    def from_(side, body):
        pl.when((has_down, has_up)[side])(body)

    loads = [
        pltpu.make_async_copy(src, dst, own.at[i])
        for i, (src, dst) in enumerate((
            (state.at[:, pl.ds(pl.multiple_of(me * 16, 16), 16), :], cols.at[0]),
            (lists_in, lists),
            (counts_in, counts),
            (obs, raw.at[1, 0]),
            (value, vp.at[1, 0]),
            (precision, vp.at[1, 1]),
        ))
    ]
    for load in loads:
        load.start()

    barrier = pltpu.get_barrier_semaphore()
    near = [(s, ((z + d) % NZ) * 2 + c) for d in (1, 2, NZ - 2, NZ - 1)]
    near += [(s, sibling)]

    def greet(peer):
        pl.semaphore_signal(barrier, inc=1, device_id=peer, device_id_type=MESH)

    for peer in near:
        greet(peer)
    toward(0, lambda: greet((up, me)))
    toward(1, lambda: greet((down, me)))
    pl.semaphore_wait(barrier, len(near) + 1 + (s + NSP - 1) // NSP - (s + 1) // NSP)

    def rcopy(src, dst, ss, rs, device):
        return pltpu.make_async_remote_copy(
            src_ref=src, dst_ref=dst, send_sem=ss, recv_sem=rs, device_id=device, device_id_type=MESH
        )

    def hop(side, far, k):
        d = 2 * k + 1 + far
        now, then = ((16 - 2 * k) % 16, 16 - d) if side == 0 else (2 * k, d)
        sems = (r1s, r1r) if far == 0 else (r2s, r2r)
        dz = (1 + far) if side == 0 else NZ - 1 - far
        peer = ((z + dz) % NZ) * 2 + c
        return rcopy(
            raw.at[1, 2 * now], raw.at[1, 2 * then], sems[0].at[side, k], sems[1].at[side, k], (s, peer)
        )

    def across(u):
        return rcopy(raw.at[1, 2 * u], raw.at[1, 2 * u + 1], sbs.at[u], sbr.at[u], (s, sibling))

    def halo(side, u):
        dst = raw.at[2 * side, 2 * u]
        return rcopy(raw.at[1, 2 * u], dst, has.at[side, u], har.at[side, u], ((up, down)[side], me))

    def halo_across(side, u):
        tile = 2 * side
        return rcopy(
            raw.at[tile, 2 * u], raw.at[tile, 2 * u + 1], shs.at[side, u], shr.at[side, u], (s, sibling)
        )

    def rim(side):
        return rcopy(vp.at[1], vp.at[2 * side], vps.at[side], vpr.at[side], ((up, down)[side], me))

    def far(j):
        return (8 + ((j + 1) // 2) * (2 * ((j + 1) % 2) - 1)) % 16

    def place(u, p):
        core = c if p == 0 else 1 - c
        return 2 * ((z + u) % NZ) + core

    def rows_of(member):
        return pl.ds(pl.multiple_of(member * 16, 16), 16)

    def send_state(u, p):
        target = place(u, p)
        slot = 2 * ((16 - u) % 16) + p
        return rcopy(
            state.at[:, rows_of(target), :], cols.at[slot], s1.at[2 * u + p], r1.at[slot], (s, target)
        )

    def send_result(u, p):
        target = place(u, p)
        slot = 2 * ((16 - u) % 16) + p
        return rcopy(
            outb.at[2 * u + p], out.at[:, rows_of(me), :], s2.at[2 * u + p], r2.at[slot], (s, target)
        )

    def spread(u):
        across(u).start()
        for side in range(2):
            toward(side, lambda side=side: halo(side, u).start())

    def relay(u):
        for side in range(2):

            def on(side=side):
                halo(side, u).wait_recv()
                halo_across(side, u).start()

            from_(side, on)

    def scatter(d, p):
        if p == 1:
            across(d).wait_recv()
        send_state(d, p).start()
        if d < 8:
            if p == 1:
                across(16 - d).wait_recv()
            send_state(16 - d, p).start()

    def sched(i):
        for d, p in SCHED[i]:
            scatter(d, p)

    for load in loads[3:]:
        load.wait()
    for side in range(2):
        hop(side, 1, 0).start()
    for side in range(2):
        hop(side, 0, 0).start()
    spread(0)
    for side in range(2):
        toward(side, lambda side=side: rim(side).start())
    sched(0)
    for k in range(1, 4):
        for side in range(2):
            hop(side, 1, k - 1).wait_recv()
            if k < 3 or side == 0:
                hop(side, 1, k).start()
        for side in range(2):
            hop(side, 0, k).start()
        spread(16 - 2 * k)
        spread(2 * k)
        for side in range(2):
            hop(side, 0, k - 1).wait_recv()
            spread((17 - 2 * k, 2 * k - 1)[side])
        if k == 1:
            relay(0)
        else:
            for d in (2 * k - 3, 2 * k - 2):
                relay(16 - d)
                relay(d)
        sched(k)
    for side in range(2):
        hop(side, 0, 3).wait_recv()
        spread((9, 7)[side])
    hop(0, 1, 3).wait_recv()
    spread(8)
    sched(4)
    across(0).wait_recv()
    send_state(0, 1).start()
    for d in (5, 6, 7, 8):
        relay(16 - d)
        if d < 8:
            relay(d)
    sched(5)

    loads[1].wait()
    loads[2].wait()
    anomalies(1, raw, vp, stage, anom, prec, inno)
    for side in range(2):

        def rim_tile(side=side):
            loop(0, 16, lambda u: halo_across(side, u).wait_recv())
            rim(side).wait_recv()
            anomalies(2 * side, raw, vp, stage, anom, prec, inno)

        from_(side, rim_tile)
    pl.when(s == 0)(lambda: no_tile(0, anom, prec, inno))
    pl.when(s == NSP - 1)(lambda: no_tile(2, anom, prec, inno))
    systems(lists, counts, anom, prec, inno, t_ref, f_ref)
    weights(t_ref, f_ref, p_ref, z_ref, w_ref)

    def unpack(u):
        for p in range(2):
            rows = cols[2 * u + p].astype(F32).reshape(128, 128)
            stage[pl.ds(pl.multiple_of(u * 256 + p * 128, 128), 128), :] = rows
        members = pl.ds(pl.multiple_of(u * 16, 16), 16)
        for g in range(NG):
            for r in range(4):
                rows = stage[pl.ds(u * 256 + 4 * g + r, 16, stride=16), :]
                xb[g, members, r * 128 : (r + 1) * 128] = rows.astype(BF)

    def await_state(slot):
        rcopy(
            state.at[:, pl.ds(0, 16), :], cols.at[slot], s1.at[slot], r1.at[slot], (s, sibling)
        ).wait_recv()

    loads[0].wait()
    await_state(1)
    unpack(0)

    def arrive(j):
        u = far(14 - j)
        await_state(2 * u)
        await_state(2 * u + 1)
        unpack(u)

    loop(0, 15, arrive)

    def apply(part):
        far_of = [far(4 * part + i) for i in range(4)]
        for g in range(NG):
            left = [
                w_ref[g, h, pl.ds(pl.multiple_of(u * 16, 16), 16), :] for h in range(2) for u in far_of
            ]
            both = dot(jnp.concatenate(left, 0), xb[g])
            done = both[:64] + both[64:]
            for r in range(4):
                stage2[pl.ds(4 * g + r, 64, stride=16), :] = done[:, r * 128 : (r + 1) * 128]
        for i, u in enumerate(far_of):
            for p in range(2):
                rows = stage2[pl.ds((2 * i + p) * 128, 128), :]
                outb[2 * u + p] = rows.reshape(8, 16, 128).astype(BF)
                if i == 3 and p == 0:

                    @pl.when(part < 3)
                    def _():
                        send_result(u, p).start()
                else:
                    send_result(u, p).start()

    loop(0, 4, apply)
    own_out = pltpu.make_async_copy(outb.at[0], out.at[:, rows_of(me), :], own.at[6])
    own_out.start()

    def settle(slot):
        rcopy(
            outb.at[slot], out.at[:, pl.ds(0, 16), :], s2.at[slot], r2.at[slot], (s, sibling)
        ).wait()
        rcopy(
            state.at[:, pl.ds(0, 16), :], cols.at[slot], s1.at[slot], r1.at[slot], (s, sibling)
        ).wait_send()

    loop(1, 32, settle)
    own_out.wait()

    for side in range(2):
        for k in range(4):
            hop(side, 0, k).wait_send()
            if side == 0 or k < 3:
                hop(side, 1, k).wait_send()

    def sent_wide(u):
        across(u).wait_send()
        for side in range(2):
            toward(side, lambda side=side: halo(side, u).wait_send())
            from_(side, lambda side=side: halo_across(side, u).wait_send())

    loop(0, 16, sent_wide)
    for side in range(2):
        toward(side, lambda side=side: rim(side).wait_send())


def per_device(state, obs_prior, obs_value, obs_precision, block_lists, list_counts):
    anywhere = pl.BlockSpec(memory_space=pl.ANY)
    dma = pltpu.SemaphoreType.DMA
    return pl.pallas_call(
        kernel,
        out_shape=jax.ShapeDtypeStruct(state.shape, state.dtype),
        in_specs=[pl.BlockSpec(memory_space=pltpu.HBM)] * 6,
        out_specs=anywhere,
        scratch_shapes=[
            pltpu.SMEM((NG, 16), jnp.int32),
            pltpu.SMEM((NG,), jnp.int32),
            pltpu.VMEM((3, 32, 8, 16, 128), BF),
            pltpu.VMEM((3, 2, 16, 128), F32),
            pltpu.VMEM((4096, 128), F32),
            pltpu.VMEM((48, MEM, 128), BF),
            pltpu.VMEM((48, 1, 128), F32),
            pltpu.VMEM((48, 1, 128), F32),
            pltpu.VMEM((NG, MEM, MEM), F32),
            pltpu.VMEM((NG, 16, MEM), F32),
            pltpu.VMEM((NG, 2, MEM, MEM), BF),
            pltpu.VMEM((NG, 2, MEM, MEM), BF),
            pltpu.VMEM((NG, 2, MEM, MEM), BF),
            pltpu.VMEM((32, 8, 16, 128), BF),
            pltpu.VMEM((NG, MEM, 512), BF),
            pltpu.VMEM((1024, 128), F32),
            pltpu.VMEM((32, 8, 16, 128), BF),
            dma((2, 4)), dma((2, 4)), dma((2, 4)), dma((2, 4)), dma((16,)), dma((16,)),
            dma((2, 16)), dma((2, 16)), dma((2, 16)), dma((2, 16)), dma((2,)), dma((2,)),
            dma((32,)), dma((32,)), dma((32,)), dma((32,)), dma((7,)),
        ],
        compiler_params=pltpu.CompilerParams(
            collective_id=0, has_side_effects=True, vmem_limit_bytes=62 << 20
        ),
        name="analysis",
    )(block_lists, list_counts, state, obs_prior, obs_value, obs_precision)


def solution(mesh):
    in_specs = (
        P("member", "space", None),
        P("member", "space", None),
        P("space", None),
        P("space", None),
        P(("space", "member"), None),
        P(("space", "member")),
    )
    out_specs = P("member", "space", None)
    return jax.shard_map(
        per_device, mesh=mesh, in_specs=in_specs, out_specs=out_specs, check_vma=False
    )
```

```python
import math

import jax
import jax.numpy as jnp
from jax import lax
from jax.experimental import pallas as pl
from jax.experimental.pallas import tpu as pltpu
from jax.sharding import PartitionSpec as P

MESH = pl.DeviceIdType.MESH
BF, F32 = jnp.bfloat16, jnp.float32
NS_ITERS = 6
NG = 4
MEM = 256
NZ = 16
NSP = 16
SCHED = (
    ((1, 0), (2, 0)),
    ((2, 1),),
    ((3, 0), (4, 0)),
    ((4, 1), (5, 0)),
    ((6, 0), (5, 1)),
)
REST = (
    ((8, 0), (7, 0), (8, 1), (7, 1), (6, 1), (3, 1), (1, 1)),
    ((8, 1), (7, 1), (6, 1), (3, 1), (1, 1), (8, 0), (7, 0)),
)


def split(x):
    high = x.astype(BF)
    return high, (x - high.astype(F32)).astype(BF)


def dot(a, b):
    return lax.dot_general(a, b, (((1,), (0,)), ((), ())), preferred_element_type=F32)


def dot3(a, b):
    (ah, al), (bh, bl) = a, b
    return dot(jnp.concatenate([ah, al, ah], 1), jnp.concatenate([bh, bh, bl], 0))


def eye():
    rows = lax.broadcasted_iota(jnp.int32, (MEM, MEM), 0)
    return (rows == lax.broadcasted_iota(jnp.int32, (MEM, MEM), 1)).astype(F32)


def loop(low, high, body):
    def step(i, carry):
        body(i)
        return carry

    lax.fori_loop(low, high, step, 0)


def anomalies(tile, raw, vp, stage, anom, prec, inno):
    def add(slot, total):
        return total + jnp.sum(raw[tile, slot].astype(F32), axis=0)

    mean = lax.fori_loop(0, 32, add, jnp.zeros((16, 128), F32)) * (1.0 / MEM)

    def centre(slot):
        rows = raw[tile, slot].astype(F32) - mean[None]
        stage[pl.ds(pl.multiple_of(slot * 128, 128), 128), :] = rows.reshape(128, 128)

    loop(0, 32, centre)

    def pick(b):
        anom[tile * 16 + b] = stage[pl.ds(b, MEM, stride=16), :].astype(BF)

    loop(0, 16, pick)
    innovation = vp[tile, 0] - mean
    precision = vp[tile, 1]
    for b in range(16):
        inno[tile * 16 + b] = innovation[b : b + 1]
        prec[tile * 16 + b] = precision[b : b + 1]


def no_tile(tile, anom, prec, inno):
    def clear(b):
        anom[tile * 16 + b] = jnp.zeros((MEM, 128), BF)
        inno[tile * 16 + b] = jnp.zeros((1, 128), F32)
        prec[tile * 16 + b] = jnp.zeros((1, 128), F32)

    loop(0, 16, clear)


def systems(lists, counts, anom, prec, inno, t_ref, f_ref):
    def group(g):
        count = counts[g]
        ys, ss, ws = [], [], []
        for e in range(16):
            b = lists[g, e]
            y = anom[b]
            r = prec[b] * jnp.where(e < count, 1.0, 0.0).astype(F32)
            ys.append(y)
            ss.append((y.astype(F32) * r).astype(BF))
            ws.append(jnp.broadcast_to((r * inno[b]).astype(BF), (16, 128)))
        left = jnp.concatenate([jnp.concatenate(ss, 1), jnp.concatenate(ws, 1)], 0)
        total = lax.dot_general(
            left, jnp.concatenate(ys, 1), (((1,), (1,)), ((), ())), preferred_element_type=F32
        )
        t_ref[g] = total[:MEM] + (MEM - 1.0) * eye()
        f_ref[g] = total[MEM:]

    def two(i):
        group(2 * i)
        group(2 * i + 1)

    loop(0, NG // 2, two)


def weights(t_ref, f_ref, p_ref, z_ref, w_ref):
    groups = range(NG)

    def load(ref):
        return [(ref[g, 0], ref[g, 1]) for g in groups]

    def store(ref, values):
        for g in groups:
            ref[g, 0], ref[g, 1] = split(values[g])

    systems_ = [t_ref[g] for g in groups]
    norms = [jnp.sqrt(jnp.sum(t * t, keepdims=True)) for t in systems_]
    iterates = [t / norm for t, norm in zip(systems_, norms)]
    factors = [1.5 * eye() - 0.5 * iterate for iterate in iterates]
    store(p_ref, [dot3(split(p), split(f)) for p, f in zip(iterates, factors)])
    store(z_ref, factors)

    def sweep(final):
        zs, ps = load(z_ref), load(p_ref)
        products = [dot3(z, p) for z, p in zip(zs, ps)]
        factors = [split(1.5 * eye() - 0.5 * product) for product in products]
        if not final:
            next_p = [dot3(p, f) for p, f in zip(ps, factors)]
        next_z = [dot3(f, z) for f, z in zip(factors, zs)]
        if not final:
            store(p_ref, next_p)
        store(z_ref, next_z)

    loop(0, NS_ITERS - 2, lambda i: sweep(False))
    sweep(True)

    zs = load(z_ref)
    halves = [split(dot3(split(f_ref[g]), zs[g])) for g in groups]
    means = [dot3(halves[g], zs[g])[0:1] / norms[g] for g in groups]
    for g in groups:
        high, low = zs[g]
        w = (high.astype(F32) + low.astype(F32)) * (math.sqrt(MEM - 1.0) / jnp.sqrt(norms[g])) + means[g]
        w = w + (1.0 - jnp.sum(w, axis=1, keepdims=True)) * (1.0 / MEM)
        w_ref[g, 0], w_ref[g, 1] = split(w)


def kernel(
    lists_in, counts_in, state, obs, value, precision, out,
    lists, counts, raw, vp, stage, anom, prec, inno, t_ref, f_ref, p_ref, z_ref, w_ref, cols, xb, stage2, outb,
    r1s, r1r, r2s, r2r, sbs, sbr, has, har, shs, shr, vps, vpr, s1, r1, s2, r2, own,
):
    s, me = lax.axis_index("space"), lax.axis_index("member")
    z, c = me // 2, me % 2
    sibling = z * 2 + 1 - c
    up, down = (s + 1) % NSP, (s + NSP - 1) % NSP
    has_up, has_down = s < NSP - 1, s > 0

    def toward(side, body):
        pl.when((has_up, has_down)[side])(body)

    def from_(side, body):
        pl.when((has_down, has_up)[side])(body)

    loads = [
        pltpu.make_async_copy(src, dst, own.at[i])
        for i, (src, dst) in enumerate((
            (state.at[:, pl.ds(pl.multiple_of(me * 16, 16), 16), :], cols.at[0]),
            (lists_in, lists),
            (counts_in, counts),
            (obs, raw.at[1, 0]),
            (value, vp.at[1, 0]),
            (precision, vp.at[1, 1]),
        ))
    ]
    for load in loads:
        load.start()

    barrier = pltpu.get_barrier_semaphore()
    near = [(s, ((z + d) % NZ) * 2 + c) for d in (1, 2, NZ - 2, NZ - 1)]
    near += [(s, sibling)]

    def greet(peer):
        pl.semaphore_signal(barrier, inc=1, device_id=peer, device_id_type=MESH)

    for peer in near:
        greet(peer)
    toward(0, lambda: greet((up, me)))
    toward(1, lambda: greet((down, me)))
    pl.semaphore_wait(barrier, len(near) + 1 + (s + NSP - 1) // NSP - (s + 1) // NSP)

    def rcopy(src, dst, ss, rs, device):
        return pltpu.make_async_remote_copy(
            src_ref=src, dst_ref=dst, send_sem=ss, recv_sem=rs, device_id=device, device_id_type=MESH
        )

    def hop(side, far, k):
        d = 2 * k + 1 + far
        now, then = ((16 - 2 * k) % 16, 16 - d) if side == 0 else (2 * k, d)
        sems = (r1s, r1r) if far == 0 else (r2s, r2r)
        dz = (1 + far) if side == 0 else NZ - 1 - far
        peer = ((z + dz) % NZ) * 2 + c
        return rcopy(
            raw.at[1, 2 * now], raw.at[1, 2 * then], sems[0].at[side, k], sems[1].at[side, k], (s, peer)
        )

    def across(u):
        return rcopy(raw.at[1, 2 * u], raw.at[1, 2 * u + 1], sbs.at[u], sbr.at[u], (s, sibling))

    def halo(side, u):
        dst = raw.at[2 * side, 2 * u]
        return rcopy(raw.at[1, 2 * u], dst, has.at[side, u], har.at[side, u], ((up, down)[side], me))

    def halo_across(side, u):
        tile = 2 * side
        return rcopy(
            raw.at[tile, 2 * u], raw.at[tile, 2 * u + 1], shs.at[side, u], shr.at[side, u], (s, sibling)
        )

    def rim(side):
        return rcopy(vp.at[1], vp.at[2 * side], vps.at[side], vpr.at[side], ((up, down)[side], me))

    def far(j):
        return (8 + ((j + 1) // 2) * (2 * ((j + 1) % 2) - 1)) % 16

    def place(u, p):
        core = c if p == 0 else 1 - c
        return 2 * ((z + u) % NZ) + core

    def rows_of(member):
        return pl.ds(pl.multiple_of(member * 16, 16), 16)

    def send_state(u, p):
        target = place(u, p)
        slot = 2 * ((16 - u) % 16) + p
        return rcopy(
            state.at[:, rows_of(target), :], cols.at[slot], s1.at[2 * u + p], r1.at[slot], (s, target)
        )

    def send_result(u, p):
        target = place(u, p)
        slot = 2 * ((16 - u) % 16) + p
        return rcopy(
            outb.at[2 * u + p], out.at[:, rows_of(me), :], s2.at[2 * u + p], r2.at[slot], (s, target)
        )

    def spread(u):
        across(u).start()
        for side in range(2):
            toward(side, lambda side=side: halo(side, u).start())

    def relay(u):
        for side in range(2):

            def on(side=side):
                halo(side, u).wait_recv()
                halo_across(side, u).start()

            from_(side, on)

    def scatter(d, p):
        if p == 1:
            across(d).wait_recv()
        send_state(d, p).start()
        if d < 8:
            if p == 1:
                across(16 - d).wait_recv()
            send_state(16 - d, p).start()

    def sched(i):
        for d, p in SCHED[i]:
            scatter(d, p)

    for load in loads[3:]:
        load.wait()
    for side in range(2):
        hop(side, 1, 0).start()
    for side in range(2):
        hop(side, 0, 0).start()
    spread(0)
    for side in range(2):
        toward(side, lambda side=side: rim(side).start())
    sched(0)
    for k in range(1, 4):
        for side in range(2):
            hop(side, 1, k - 1).wait_recv()
            if k < 3 or side == 0:
                hop(side, 1, k).start()
        for side in range(2):
            hop(side, 0, k).start()
        spread(16 - 2 * k)
        spread(2 * k)
        for side in range(2):
            hop(side, 0, k - 1).wait_recv()
            spread((17 - 2 * k, 2 * k - 1)[side])
        if k == 1:
            relay(0)
        else:
            for d in (2 * k - 3, 2 * k - 2):
                relay(16 - d)
                relay(d)
        sched(k)
    for side in range(2):
        hop(side, 0, 3).wait_recv()
        spread((9, 7)[side])
    hop(0, 1, 3).wait_recv()
    spread(8)
    sched(4)
    across(0).wait_recv()
    send_state(0, 1).start()
    for d in (5, 6, 7, 8):
        relay(16 - d)
        if d < 8:
            relay(d)
    for core in range(2):

        def rest(core=core):
            for d, p in REST[core]:
                scatter(d, p)

        pl.when(c == core)(rest)

    loads[1].wait()
    loads[2].wait()
    anomalies(1, raw, vp, stage, anom, prec, inno)
    for side in range(2):

        def rim_tile(side=side):
            loop(0, 16, lambda u: halo_across(side, u).wait_recv())
            rim(side).wait_recv()
            anomalies(2 * side, raw, vp, stage, anom, prec, inno)

        from_(side, rim_tile)
    pl.when(s == 0)(lambda: no_tile(0, anom, prec, inno))
    pl.when(s == NSP - 1)(lambda: no_tile(2, anom, prec, inno))
    systems(lists, counts, anom, prec, inno, t_ref, f_ref)
    weights(t_ref, f_ref, p_ref, z_ref, w_ref)

    def unpack(u):
        for p in range(2):
            rows = cols[2 * u + p].astype(F32).reshape(128, 128)
            stage[pl.ds(pl.multiple_of(u * 256 + p * 128, 128), 128), :] = rows
        members = pl.ds(pl.multiple_of(u * 16, 16), 16)
        for g in range(NG):
            for r in range(4):
                rows = stage[pl.ds(u * 256 + 4 * g + r, 16, stride=16), :]
                xb[g, members, r * 128 : (r + 1) * 128] = rows.astype(BF)

    def await_state(slot):
        rcopy(
            state.at[:, pl.ds(0, 16), :], cols.at[slot], s1.at[slot], r1.at[slot], (s, sibling)
        ).wait_recv()

    loads[0].wait()
    await_state(1)
    unpack(0)

    def arrive(j):
        u = far(14 - j)
        await_state(2 * u)
        await_state(2 * u + 1)
        unpack(u)

    loop(0, 15, arrive)

    def apply(part):
        far_of = [far(4 * part + i) for i in range(4)]
        for g in range(NG):
            left = [
                w_ref[g, h, pl.ds(pl.multiple_of(u * 16, 16), 16), :] for h in range(2) for u in far_of
            ]
            both = dot(jnp.concatenate(left, 0), xb[g])
            done = both[:64] + both[64:]
            for r in range(4):
                stage2[pl.ds(4 * g + r, 64, stride=16), :] = done[:, r * 128 : (r + 1) * 128]
        for i, u in enumerate(far_of):
            for p in range(2):
                rows = stage2[pl.ds((2 * i + p) * 128, 128), :]
                outb[2 * u + p] = rows.reshape(8, 16, 128).astype(BF)
                if i == 3 and p == 0:

                    @pl.when(part < 3)
                    def _():
                        send_result(u, p).start()
                else:
                    send_result(u, p).start()

    loop(0, 4, apply)
    own_out = pltpu.make_async_copy(outb.at[0], out.at[:, rows_of(me), :], own.at[6])
    own_out.start()

    def settle(slot):
        rcopy(
            outb.at[slot], out.at[:, pl.ds(0, 16), :], s2.at[slot], r2.at[slot], (s, sibling)
        ).wait()
        rcopy(
            state.at[:, pl.ds(0, 16), :], cols.at[slot], s1.at[slot], r1.at[slot], (s, sibling)
        ).wait_send()

    loop(1, 32, settle)
    own_out.wait()

    for side in range(2):
        for k in range(4):
            hop(side, 0, k).wait_send()
            if side == 0 or k < 3:
                hop(side, 1, k).wait_send()

    def sent_wide(u):
        across(u).wait_send()
        for side in range(2):
            toward(side, lambda side=side: halo(side, u).wait_send())
            from_(side, lambda side=side: halo_across(side, u).wait_send())

    loop(0, 16, sent_wide)
    for side in range(2):
        toward(side, lambda side=side: rim(side).wait_send())


def per_device(state, obs_prior, obs_value, obs_precision, block_lists, list_counts):
    anywhere = pl.BlockSpec(memory_space=pl.ANY)
    dma = pltpu.SemaphoreType.DMA
    return pl.pallas_call(
        kernel,
        out_shape=jax.ShapeDtypeStruct(state.shape, state.dtype),
        in_specs=[pl.BlockSpec(memory_space=pltpu.HBM)] * 6,
        out_specs=anywhere,
        scratch_shapes=[
            pltpu.SMEM((NG, 16), jnp.int32),
            pltpu.SMEM((NG,), jnp.int32),
            pltpu.VMEM((3, 32, 8, 16, 128), BF),
            pltpu.VMEM((3, 2, 16, 128), F32),
            pltpu.VMEM((4096, 128), F32),
            pltpu.VMEM((48, MEM, 128), BF),
            pltpu.VMEM((48, 1, 128), F32),
            pltpu.VMEM((48, 1, 128), F32),
            pltpu.VMEM((NG, MEM, MEM), F32),
            pltpu.VMEM((NG, 16, MEM), F32),
            pltpu.VMEM((NG, 2, MEM, MEM), BF),
            pltpu.VMEM((NG, 2, MEM, MEM), BF),
            pltpu.VMEM((NG, 2, MEM, MEM), BF),
            pltpu.VMEM((32, 8, 16, 128), BF),
            pltpu.VMEM((NG, MEM, 512), BF),
            pltpu.VMEM((1024, 128), F32),
            pltpu.VMEM((32, 8, 16, 128), BF),
            dma((2, 4)), dma((2, 4)), dma((2, 4)), dma((2, 4)), dma((16,)), dma((16,)),
            dma((2, 16)), dma((2, 16)), dma((2, 16)), dma((2, 16)), dma((2,)), dma((2,)),
            dma((32,)), dma((32,)), dma((32,)), dma((32,)), dma((7,)),
        ],
        compiler_params=pltpu.CompilerParams(
            collective_id=0, has_side_effects=True, vmem_limit_bytes=62 << 20
        ),
        name="analysis",
    )(block_lists, list_counts, state, obs_prior, obs_value, obs_precision)


def solution(mesh):
    in_specs = (
        P("member", "space", None),
        P("member", "space", None),
        P("space", None),
        P("space", None),
        P(("space", "member"), None),
        P(("space", "member")),
    )
    out_specs = P("member", "space", None)
    return jax.shard_map(
        per_device, mesh=mesh, in_specs=in_specs, out_specs=out_specs, check_vma=False
    )
```

```python
import math

import jax
import jax.numpy as jnp
from jax import lax
from jax.experimental import pallas as pl
from jax.experimental.pallas import tpu as pltpu
from jax.sharding import PartitionSpec as P

MESH = pl.DeviceIdType.MESH
BF, F32 = jnp.bfloat16, jnp.float32
NS_ITERS = 6
NG = 4
MEM = 256
NZ = 16
NSP = 16
SCHED = (
    ((1, 0), (2, 0)),
    ((2, 1),),
    ((3, 0), (4, 0)),
    ((4, 1), (5, 0)),
    ((6, 0), (5, 1)),
)
REST = (
    ((8, 0), (7, 0), (8, 1), (7, 1), (6, 1), (3, 1), (1, 1)),
    ((8, 1), (7, 1), (6, 1), (3, 1), (1, 1), (8, 0), (7, 0)),
)


def split(x):
    high = x.astype(BF)
    return high, (x - high.astype(F32)).astype(BF)


def dot(a, b):
    return lax.dot_general(a, b, (((1,), (0,)), ((), ())), preferred_element_type=F32)


def dot3(a, b):
    (ah, al), (bh, bl) = a, b
    return dot(jnp.concatenate([ah, al, ah], 1), jnp.concatenate([bh, bh, bl], 0))


def eye():
    rows = lax.broadcasted_iota(jnp.int32, (MEM, MEM), 0)
    return (rows == lax.broadcasted_iota(jnp.int32, (MEM, MEM), 1)).astype(F32)


def loop(low, high, body):
    def step(i, carry):
        body(i)
        return carry

    lax.fori_loop(low, high, step, 0)


def anomalies(tile, raw, vp, stage, anom, prec, inno):
    def add(slot, total):
        return total + jnp.sum(raw[tile, slot].astype(F32), axis=0)

    mean = lax.fori_loop(0, 32, add, jnp.zeros((16, 128), F32)) * (1.0 / MEM)

    def centre(slot):
        rows = raw[tile, slot].astype(F32) - mean[None]
        stage[pl.ds(pl.multiple_of(slot * 128, 128), 128), :] = rows.reshape(128, 128)

    loop(0, 32, centre)

    def pick(b):
        anom[tile * 16 + b] = stage[pl.ds(b, MEM, stride=16), :].astype(BF)

    loop(0, 16, pick)
    innovation = vp[tile, 0] - mean
    precision = vp[tile, 1]
    for b in range(16):
        inno[tile * 16 + b] = innovation[b : b + 1]
        prec[tile * 16 + b] = precision[b : b + 1]


def no_tile(tile, anom, prec, inno):
    def clear(b):
        anom[tile * 16 + b] = jnp.zeros((MEM, 128), BF)
        inno[tile * 16 + b] = jnp.zeros((1, 128), F32)
        prec[tile * 16 + b] = jnp.zeros((1, 128), F32)

    loop(0, 16, clear)


def systems(lists, counts, anom, prec, inno, t_ref, f_ref):
    def group(g):
        count = counts[g]
        ys, ss, ws = [], [], []
        for e in range(16):
            b = lists[g, e]
            y = anom[b]
            r = prec[b] * jnp.where(e < count, 1.0, 0.0).astype(F32)
            ys.append(y)
            ss.append((y.astype(F32) * r).astype(BF))
            ws.append(jnp.broadcast_to((r * inno[b]).astype(BF), (16, 128)))
        left = jnp.concatenate([jnp.concatenate(ss, 1), jnp.concatenate(ws, 1)], 0)
        total = lax.dot_general(
            left, jnp.concatenate(ys, 1), (((1,), (1,)), ((), ())), preferred_element_type=F32
        )
        t_ref[g] = total[:MEM] + (MEM - 1.0) * eye()
        f_ref[g] = total[MEM:]

    def two(i):
        group(2 * i)
        group(2 * i + 1)

    loop(0, NG // 2, two)


def weights(t_ref, f_ref, p_ref, z_ref, w_ref):
    groups = range(NG)

    def load(ref):
        return [(ref[g, 0], ref[g, 1]) for g in groups]

    def store(ref, values):
        for g in groups:
            ref[g, 0], ref[g, 1] = split(values[g])

    systems_ = [t_ref[g] for g in groups]
    norms = [jnp.sqrt(jnp.sum(t * t, keepdims=True)) for t in systems_]
    iterates = [t / norm for t, norm in zip(systems_, norms)]
    factors = [1.5 * eye() - 0.5 * iterate for iterate in iterates]
    store(p_ref, [dot3(split(p), split(f)) for p, f in zip(iterates, factors)])
    store(z_ref, factors)

    def sweep(final):
        zs, ps = load(z_ref), load(p_ref)
        products = [dot3(z, p) for z, p in zip(zs, ps)]
        factors = [split(1.5 * eye() - 0.5 * product) for product in products]
        if not final:
            next_p = [dot3(p, f) for p, f in zip(ps, factors)]
        next_z = [dot3(f, z) for f, z in zip(factors, zs)]
        if not final:
            store(p_ref, next_p)
        store(z_ref, next_z)

    loop(0, NS_ITERS - 2, lambda i: sweep(False))
    sweep(True)

    zs = load(z_ref)
    halves = [split(dot3(split(f_ref[g]), zs[g])) for g in groups]
    means = [dot3(halves[g], zs[g])[0:1] / norms[g] for g in groups]
    for g in groups:
        high, low = zs[g]
        w = (high.astype(F32) + low.astype(F32)) * (math.sqrt(MEM - 1.0) / jnp.sqrt(norms[g])) + means[g]
        w = w + (1.0 - jnp.sum(w, axis=1, keepdims=True)) * (1.0 / MEM)
        w_ref[g, 0], w_ref[g, 1] = split(w)


def kernel(
    lists_in, counts_in, state, obs, value, precision, out,
    lists, counts, raw, vp, stage, anom, prec, inno, t_ref, f_ref, p_ref, z_ref, w_ref, cols, xb, stage2, outb,
    r1s, r1r, r2s, r2r, sbs, sbr, has, har, shs, shr, vps, vpr, s1, r1, s2, r2, own,
):
    s, me = lax.axis_index("space"), lax.axis_index("member")
    z, c = me // 2, me % 2
    sibling = z * 2 + 1 - c
    up, down = (s + 1) % NSP, (s + NSP - 1) % NSP
    has_up, has_down = s < NSP - 1, s > 0

    def toward(side, body):
        pl.when((has_up, has_down)[side])(body)

    def from_(side, body):
        pl.when((has_down, has_up)[side])(body)

    barrier = pltpu.get_barrier_semaphore()
    near = [(s, ((z + d) % NZ) * 2 + c) for d in (1, 2, NZ - 2, NZ - 1)]
    near += [(s, sibling)]

    def greet(peer):
        pl.semaphore_signal(barrier, inc=1, device_id=peer, device_id_type=MESH)

    for peer in near:
        greet(peer)
    toward(0, lambda: greet((up, me)))
    toward(1, lambda: greet((down, me)))

    loads = [
        pltpu.make_async_copy(src, dst, own.at[i])
        for i, (src, dst) in enumerate((
            (state.at[:, pl.ds(pl.multiple_of(me * 16, 16), 16), :], cols.at[0]),
            (lists_in, lists),
            (counts_in, counts),
            (obs, raw.at[1, 0]),
            (value, vp.at[1, 0]),
            (precision, vp.at[1, 1]),
        ))
    ]
    for load in loads:
        load.start()
    pl.semaphore_wait(barrier, len(near) + 1 + (s + NSP - 1) // NSP - (s + 1) // NSP)

    def rcopy(src, dst, ss, rs, device):
        return pltpu.make_async_remote_copy(
            src_ref=src, dst_ref=dst, send_sem=ss, recv_sem=rs, device_id=device, device_id_type=MESH
        )

    def hop(side, far, k):
        d = 2 * k + 1 + far
        now, then = ((16 - 2 * k) % 16, 16 - d) if side == 0 else (2 * k, d)
        sems = (r1s, r1r) if far == 0 else (r2s, r2r)
        dz = (1 + far) if side == 0 else NZ - 1 - far
        peer = ((z + dz) % NZ) * 2 + c
        return rcopy(
            raw.at[1, 2 * now], raw.at[1, 2 * then], sems[0].at[side, k], sems[1].at[side, k], (s, peer)
        )

    def across(u):
        return rcopy(raw.at[1, 2 * u], raw.at[1, 2 * u + 1], sbs.at[u], sbr.at[u], (s, sibling))

    def halo(side, u):
        dst = raw.at[2 * side, 2 * u]
        return rcopy(raw.at[1, 2 * u], dst, has.at[side, u], har.at[side, u], ((up, down)[side], me))

    def halo_across(side, u):
        tile = 2 * side
        return rcopy(
            raw.at[tile, 2 * u], raw.at[tile, 2 * u + 1], shs.at[side, u], shr.at[side, u], (s, sibling)
        )

    def rim(side):
        return rcopy(vp.at[1], vp.at[2 * side], vps.at[side], vpr.at[side], ((up, down)[side], me))

    def far(j):
        return (8 + ((j + 1) // 2) * (2 * ((j + 1) % 2) - 1)) % 16

    def place(u, p):
        core = c if p == 0 else 1 - c
        return 2 * ((z + u) % NZ) + core

    def rows_of(member):
        return pl.ds(pl.multiple_of(member * 16, 16), 16)

    def send_state(u, p):
        target = place(u, p)
        slot = 2 * ((16 - u) % 16) + p
        return rcopy(
            state.at[:, rows_of(target), :], cols.at[slot], s1.at[2 * u + p], r1.at[slot], (s, target)
        )

    def send_result(u, p):
        target = place(u, p)
        slot = 2 * ((16 - u) % 16) + p
        return rcopy(
            outb.at[2 * u + p], out.at[:, rows_of(me), :], s2.at[2 * u + p], r2.at[slot], (s, target)
        )

    def spread(u):
        across(u).start()
        for side in range(2):
            toward(side, lambda side=side: halo(side, u).start())

    def relay(u):
        for side in range(2):

            def on(side=side):
                halo(side, u).wait_recv()
                halo_across(side, u).start()

            from_(side, on)

    def scatter(d, p):
        if p == 1:
            across(d).wait_recv()
        send_state(d, p).start()
        if d < 8:
            if p == 1:
                across(16 - d).wait_recv()
            send_state(16 - d, p).start()

    def sched(i):
        for d, p in SCHED[i]:
            scatter(d, p)

    loads[3].wait()
    for side in range(2):
        hop(side, 1, 0).start()
    for side in range(2):
        hop(side, 0, 0).start()
    spread(0)
    loads[4].wait()
    loads[5].wait()
    for side in range(2):
        toward(side, lambda side=side: rim(side).start())
    sched(0)
    for k in range(1, 4):
        for side in range(2):
            hop(side, 1, k - 1).wait_recv()
            if k < 3 or side == 0:
                hop(side, 1, k).start()
        for side in range(2):
            hop(side, 0, k).start()
        spread(16 - 2 * k)
        spread(2 * k)
        for side in range(2):
            hop(side, 0, k - 1).wait_recv()
            spread((17 - 2 * k, 2 * k - 1)[side])
        if k == 1:
            relay(0)
        else:
            for d in (2 * k - 3, 2 * k - 2):
                relay(16 - d)
                relay(d)
        sched(k)
    for side in range(2):
        hop(side, 0, 3).wait_recv()
        spread((9, 7)[side])
    hop(0, 1, 3).wait_recv()
    spread(8)
    sched(4)
    across(0).wait_recv()
    send_state(0, 1).start()
    for d in (5, 6, 7, 8):
        relay(16 - d)
        if d < 8:
            relay(d)
    for core in range(2):

        def rest(core=core):
            for d, p in REST[core]:
                scatter(d, p)

        pl.when(c == core)(rest)

    loads[1].wait()
    loads[2].wait()
    anomalies(1, raw, vp, stage, anom, prec, inno)
    for side in range(2):

        def rim_tile(side=side):
            loop(0, 16, lambda u: halo_across(side, u).wait_recv())
            rim(side).wait_recv()
            anomalies(2 * side, raw, vp, stage, anom, prec, inno)

        from_(side, rim_tile)
    pl.when(s == 0)(lambda: no_tile(0, anom, prec, inno))
    pl.when(s == NSP - 1)(lambda: no_tile(2, anom, prec, inno))
    systems(lists, counts, anom, prec, inno, t_ref, f_ref)
    weights(t_ref, f_ref, p_ref, z_ref, w_ref)

    def unpack(u):
        for p in range(2):
            rows = cols[2 * u + p].astype(F32).reshape(128, 128)
            stage[pl.ds(pl.multiple_of(u * 256 + p * 128, 128), 128), :] = rows
        members = pl.ds(pl.multiple_of(u * 16, 16), 16)
        for g in range(NG):
            for r in range(4):
                rows = stage[pl.ds(u * 256 + 4 * g + r, 16, stride=16), :]
                xb[g, members, r * 128 : (r + 1) * 128] = rows.astype(BF)

    def await_state(slot):
        rcopy(
            state.at[:, pl.ds(0, 16), :], cols.at[slot], s1.at[slot], r1.at[slot], (s, sibling)
        ).wait_recv()

    loads[0].wait()
    await_state(1)
    unpack(0)

    def arrive(j):
        u = far(14 - j)
        await_state(2 * u)
        await_state(2 * u + 1)
        unpack(u)

    loop(0, 15, arrive)

    def apply(part):
        far_of = [far(4 * part + i) for i in range(4)]
        for g in range(NG):
            left = [
                w_ref[g, h, pl.ds(pl.multiple_of(u * 16, 16), 16), :] for h in range(2) for u in far_of
            ]
            both = dot(jnp.concatenate(left, 0), xb[g])
            done = both[:64] + both[64:]
            for r in range(4):
                stage2[pl.ds(4 * g + r, 64, stride=16), :] = done[:, r * 128 : (r + 1) * 128]
        for i, u in enumerate(far_of):
            for p in range(2):
                rows = stage2[pl.ds((2 * i + p) * 128, 128), :]
                outb[2 * u + p] = rows.reshape(8, 16, 128).astype(BF)
                if i == 3 and p == 0:

                    @pl.when(part < 3)
                    def _():
                        send_result(u, p).start()
                else:
                    send_result(u, p).start()

    loop(0, 4, apply)
    own_out = pltpu.make_async_copy(outb.at[0], out.at[:, rows_of(me), :], own.at[6])
    own_out.start()

    def settle(slot):
        rcopy(
            outb.at[slot], out.at[:, pl.ds(0, 16), :], s2.at[slot], r2.at[slot], (s, sibling)
        ).wait()
        rcopy(
            state.at[:, pl.ds(0, 16), :], cols.at[slot], s1.at[slot], r1.at[slot], (s, sibling)
        ).wait_send()

    loop(1, 32, settle)
    own_out.wait()

    for side in range(2):
        for k in range(4):
            hop(side, 0, k).wait_send()
            if side == 0 or k < 3:
                hop(side, 1, k).wait_send()

    def sent_wide(u):
        across(u).wait_send()
        for side in range(2):
            toward(side, lambda side=side: halo(side, u).wait_send())
            from_(side, lambda side=side: halo_across(side, u).wait_send())

    loop(0, 16, sent_wide)
    for side in range(2):
        toward(side, lambda side=side: rim(side).wait_send())


def per_device(state, obs_prior, obs_value, obs_precision, block_lists, list_counts):
    anywhere = pl.BlockSpec(memory_space=pl.ANY)
    dma = pltpu.SemaphoreType.DMA
    return pl.pallas_call(
        kernel,
        out_shape=jax.ShapeDtypeStruct(state.shape, state.dtype),
        in_specs=[pl.BlockSpec(memory_space=pltpu.HBM)] * 6,
        out_specs=anywhere,
        scratch_shapes=[
            pltpu.SMEM((NG, 16), jnp.int32),
            pltpu.SMEM((NG,), jnp.int32),
            pltpu.VMEM((3, 32, 8, 16, 128), BF),
            pltpu.VMEM((3, 2, 16, 128), F32),
            pltpu.VMEM((4096, 128), F32),
            pltpu.VMEM((48, MEM, 128), BF),
            pltpu.VMEM((48, 1, 128), F32),
            pltpu.VMEM((48, 1, 128), F32),
            pltpu.VMEM((NG, MEM, MEM), F32),
            pltpu.VMEM((NG, 16, MEM), F32),
            pltpu.VMEM((NG, 2, MEM, MEM), BF),
            pltpu.VMEM((NG, 2, MEM, MEM), BF),
            pltpu.VMEM((NG, 2, MEM, MEM), BF),
            pltpu.VMEM((32, 8, 16, 128), BF),
            pltpu.VMEM((NG, MEM, 512), BF),
            pltpu.VMEM((1024, 128), F32),
            pltpu.VMEM((32, 8, 16, 128), BF),
            dma((2, 4)), dma((2, 4)), dma((2, 4)), dma((2, 4)), dma((16,)), dma((16,)),
            dma((2, 16)), dma((2, 16)), dma((2, 16)), dma((2, 16)), dma((2,)), dma((2,)),
            dma((32,)), dma((32,)), dma((32,)), dma((32,)), dma((7,)),
        ],
        compiler_params=pltpu.CompilerParams(
            collective_id=0, has_side_effects=True, vmem_limit_bytes=62 << 20
        ),
        name="analysis",
    )(block_lists, list_counts, state, obs_prior, obs_value, obs_precision)


def solution(mesh):
    in_specs = (
        P("member", "space", None),
        P("member", "space", None),
        P("space", None),
        P("space", None),
        P(("space", "member"), None),
        P(("space", "member")),
    )
    out_specs = P("member", "space", None)
    return jax.shard_map(
        per_device, mesh=mesh, in_specs=in_specs, out_specs=out_specs, check_vma=False
    )
```

```python
import math

import jax
import jax.numpy as jnp
from jax import lax
from jax.experimental import pallas as pl
from jax.experimental.pallas import tpu as pltpu
from jax.sharding import PartitionSpec as P

MESH = pl.DeviceIdType.MESH
BF, F32 = jnp.bfloat16, jnp.float32
NS_ITERS = 6
NG = 4
MEM = 256
NZ = 16
NSP = 16
SCHED = (
    ((1, 0), (2, 0)),
    ((2, 1),),
    ((3, 0), (4, 0)),
    ((4, 1), (5, 0)),
    ((6, 0), (5, 1)),
)
REST = (
    ((8, 0), (7, 0), (8, 1), (7, 1), (6, 1), (3, 1), (1, 1)),
    ((8, 1), (7, 1), (6, 1), (3, 1), (1, 1), (8, 0), (7, 0)),
)


def split(x):
    high = x.astype(BF)
    return high, (x - high.astype(F32)).astype(BF)


def dot(a, b):
    return lax.dot_general(a, b, (((1,), (0,)), ((), ())), preferred_element_type=F32)


def dot3(a, b):
    (ah, al), (bh, bl) = a, b
    return dot(jnp.concatenate([ah, al, ah], 1), jnp.concatenate([bh, bh, bl], 0))


def eye():
    rows = lax.broadcasted_iota(jnp.int32, (MEM, MEM), 0)
    return (rows == lax.broadcasted_iota(jnp.int32, (MEM, MEM), 1)).astype(F32)


def loop(low, high, body):
    def step(i, carry):
        body(i)
        return carry

    lax.fori_loop(low, high, step, 0)


def anomalies(tile, raw, vp, stage, anom, prec, inno):
    def add(slot, total):
        return total + jnp.sum(raw[tile, slot].astype(F32), axis=0)

    mean = lax.fori_loop(0, 32, add, jnp.zeros((16, 128), F32)) * (1.0 / MEM)

    def centre(slot):
        rows = raw[tile, slot].astype(F32) - mean[None]
        stage[pl.ds(pl.multiple_of(slot * 128, 128), 128), :] = rows.reshape(128, 128)

    loop(0, 32, centre)

    def pick(b):
        anom[tile * 16 + b] = stage[pl.ds(b, MEM, stride=16), :].astype(BF)

    loop(0, 16, pick)
    innovation = vp[tile, 0] - mean
    precision = vp[tile, 1]
    for b in range(16):
        inno[tile * 16 + b] = innovation[b : b + 1]
        prec[tile * 16 + b] = precision[b : b + 1]


def no_tile(tile, anom, prec, inno):
    def clear(b):
        anom[tile * 16 + b] = jnp.zeros((MEM, 128), BF)
        inno[tile * 16 + b] = jnp.zeros((1, 128), F32)
        prec[tile * 16 + b] = jnp.zeros((1, 128), F32)

    loop(0, 16, clear)


def systems(lists, counts, anom, prec, inno, t_ref, f_ref):
    def group(g):
        count = counts[g]
        ys, ss, ws = [], [], []
        for e in range(16):
            b = lists[g, e]
            y = anom[b]
            r = prec[b] * jnp.where(e < count, 1.0, 0.0).astype(F32)
            ys.append(y)
            ss.append((y.astype(F32) * r).astype(BF))
            ws.append(jnp.broadcast_to((r * inno[b]).astype(BF), (16, 128)))
        left = jnp.concatenate([jnp.concatenate(ss, 1), jnp.concatenate(ws, 1)], 0)
        total = lax.dot_general(
            left, jnp.concatenate(ys, 1), (((1,), (1,)), ((), ())), preferred_element_type=F32
        )
        t_ref[g] = total[:MEM] + (MEM - 1.0) * eye()
        f_ref[g] = total[MEM:]

    def two(i):
        group(2 * i)
        group(2 * i + 1)

    loop(0, NG // 2, two)


def weights(t_ref, f_ref, p_ref, z_ref, w_ref):
    groups = range(NG)

    def load(ref):
        return [(ref[g, 0], ref[g, 1]) for g in groups]

    def store(ref, values):
        for g in groups:
            ref[g, 0], ref[g, 1] = split(values[g])

    systems_ = [t_ref[g] for g in groups]
    norms = [jnp.sqrt(jnp.sum(t * t, keepdims=True)) for t in systems_]
    iterates = [t / norm for t, norm in zip(systems_, norms)]
    factors = [1.5 * eye() - 0.5 * iterate for iterate in iterates]
    store(p_ref, [dot3(split(p), split(f)) for p, f in zip(iterates, factors)])
    store(z_ref, factors)

    def sweep(final):
        zs, ps = load(z_ref), load(p_ref)
        products = [dot3(z, p) for z, p in zip(zs, ps)]
        factors = [split(1.5 * eye() - 0.5 * product) for product in products]
        if not final:
            next_p = [dot3(p, f) for p, f in zip(ps, factors)]
        next_z = [dot3(f, z) for f, z in zip(factors, zs)]
        if not final:
            store(p_ref, next_p)
        store(z_ref, next_z)

    loop(0, NS_ITERS - 2, lambda i: sweep(False))
    sweep(True)

    zs = load(z_ref)
    halves = [split(dot3(split(f_ref[g]), zs[g])) for g in groups]
    means = [dot3(halves[g], zs[g])[0:1] / norms[g] for g in groups]
    for g in groups:
        high, low = zs[g]
        w = (high.astype(F32) + low.astype(F32)) * (math.sqrt(MEM - 1.0) / jnp.sqrt(norms[g])) + means[g]
        w = w + (1.0 - jnp.sum(w, axis=1, keepdims=True)) * (1.0 / MEM)
        w_ref[g, 0], w_ref[g, 1] = split(w)


def kernel(
    lists_in, counts_in, state, obs, value, precision, out,
    lists, counts, raw, vp, stage, anom, prec, inno, t_ref, f_ref, p_ref, z_ref, w_ref, cols, xb, stage2, outb,
    r1s, r1r, r2s, r2r, sbs, sbr, has, har, shs, shr, vps, vpr, s1, r1, s2, r2, own,
):
    s, me = lax.axis_index("space"), lax.axis_index("member")
    z, c = me // 2, me % 2
    sibling = z * 2 + 1 - c
    up, down = (s + 1) % NSP, (s + NSP - 1) % NSP
    has_up, has_down = s < NSP - 1, s > 0

    def toward(side, body):
        pl.when((has_up, has_down)[side])(body)

    def from_(side, body):
        pl.when((has_down, has_up)[side])(body)

    barrier = pltpu.get_barrier_semaphore()
    near = [(s, ((z + d) % NZ) * 2 + c) for d in (1, 2, NZ - 2, NZ - 1)]
    near += [(s, sibling)]

    def greet(peer):
        pl.semaphore_signal(barrier, inc=1, device_id=peer, device_id_type=MESH)

    for peer in near:
        greet(peer)
    toward(0, lambda: greet((up, me)))
    toward(1, lambda: greet((down, me)))

    loads = [
        pltpu.make_async_copy(src, dst, own.at[i])
        for i, (src, dst) in enumerate((
            (state.at[:, pl.ds(pl.multiple_of(me * 16, 16), 16), :], cols.at[0]),
            (lists_in, lists),
            (counts_in, counts),
            (obs, raw.at[1, 0]),
            (value, vp.at[1, 0]),
            (precision, vp.at[1, 1]),
        ))
    ]
    for load in loads:
        load.start()
    pl.semaphore_wait(barrier, len(near) + 1 + (s + NSP - 1) // NSP - (s + 1) // NSP)

    def rcopy(src, dst, ss, rs, device):
        return pltpu.make_async_remote_copy(
            src_ref=src, dst_ref=dst, send_sem=ss, recv_sem=rs, device_id=device, device_id_type=MESH
        )

    def hop(side, far, k):
        d = 2 * k + 1 + far
        now, then = ((16 - 2 * k) % 16, 16 - d) if side == 0 else (2 * k, d)
        sems = (r1s, r1r) if far == 0 else (r2s, r2r)
        dz = (1 + far) if side == 0 else NZ - 1 - far
        peer = ((z + dz) % NZ) * 2 + c
        return rcopy(
            raw.at[1, 2 * now], raw.at[1, 2 * then], sems[0].at[side, k], sems[1].at[side, k], (s, peer)
        )

    def across(u):
        return rcopy(raw.at[1, 2 * u], raw.at[1, 2 * u + 1], sbs.at[u], sbr.at[u], (s, sibling))

    def halo(side, u):
        dst = raw.at[2 * side, 2 * u]
        return rcopy(raw.at[1, 2 * u], dst, has.at[side, u], har.at[side, u], ((up, down)[side], me))

    def halo_across(side, u):
        tile = 2 * side
        return rcopy(
            raw.at[tile, 2 * u], raw.at[tile, 2 * u + 1], shs.at[side, u], shr.at[side, u], (s, sibling)
        )

    def rim(side):
        return rcopy(vp.at[1], vp.at[2 * side], vps.at[side], vpr.at[side], ((up, down)[side], me))

    def far(j):
        return (8 + ((j + 1) // 2) * (2 * ((j + 1) % 2) - 1)) % 16

    def place(u, p):
        core = c if p == 0 else 1 - c
        return 2 * ((z + u) % NZ) + core

    def rows_of(member):
        return pl.ds(pl.multiple_of(member * 16, 16), 16)

    def send_state(u, p):
        target = place(u, p)
        slot = 2 * ((16 - u) % 16) + p
        return rcopy(
            state.at[:, rows_of(target), :], cols.at[slot], s1.at[2 * u + p], r1.at[slot], (s, target)
        )

    def send_result(u, p):
        target = place(u, p)
        slot = 2 * ((16 - u) % 16) + p
        return rcopy(
            outb.at[2 * u + p], out.at[:, rows_of(me), :], s2.at[2 * u + p], r2.at[slot], (s, target)
        )

    def spread(u):
        across(u).start()
        for side in range(2):
            toward(side, lambda side=side: halo(side, u).start())

    def relay(u):
        for side in range(2):

            def on(side=side):
                halo(side, u).wait_recv()
                halo_across(side, u).start()

            from_(side, on)

    def scatter(d, p):
        if p == 1:
            across(d).wait_recv()
        send_state(d, p).start()
        if d < 8:
            if p == 1:
                across(16 - d).wait_recv()
            send_state(16 - d, p).start()

    def sched(i):
        for d, p in SCHED[i]:
            scatter(d, p)

    loads[3].wait()
    for side in range(2):
        hop(side, 1, 0).start()
    for side in range(2):
        hop(side, 0, 0).start()
    spread(0)
    loads[4].wait()
    loads[5].wait()
    for side in range(2):
        toward(side, lambda side=side: rim(side).start())
    sched(0)
    for k in range(1, 4):
        for side in range(2):
            hop(side, 1, k - 1).wait_recv()
            if k < 3 or side == 0:
                hop(side, 1, k).start()
        for side in range(2):
            hop(side, 0, k).start()
        spread(16 - 2 * k)
        spread(2 * k)
        for side in range(2):
            hop(side, 0, k - 1).wait_recv()
            spread((17 - 2 * k, 2 * k - 1)[side])
        if k == 1:
            relay(0)
        else:
            for d in (2 * k - 3, 2 * k - 2):
                relay(16 - d)
                relay(d)
        sched(k)
    for side in range(2):
        hop(side, 0, 3).wait_recv()
        spread((9, 7)[side])
    hop(0, 1, 3).wait_recv()
    spread(8)
    sched(4)
    across(0).wait_recv()
    send_state(0, 1).start()
    for d in (5, 6, 7, 8):
        relay(16 - d)
        if d < 8:
            relay(d)
    for core in range(2):

        def rest(core=core):
            for d, p in REST[core]:
                scatter(d, p)

        pl.when(c == core)(rest)

    loads[1].wait()
    loads[2].wait()
    anomalies(1, raw, vp, stage, anom, prec, inno)
    for side in range(2):

        def rim_tile(side=side):
            loop(0, 16, lambda u: halo_across(side, u).wait_recv())
            rim(side).wait_recv()
            anomalies(2 * side, raw, vp, stage, anom, prec, inno)

        from_(side, rim_tile)
    pl.when(s == 0)(lambda: no_tile(0, anom, prec, inno))
    pl.when(s == NSP - 1)(lambda: no_tile(2, anom, prec, inno))
    systems(lists, counts, anom, prec, inno, t_ref, f_ref)
    weights(t_ref, f_ref, p_ref, z_ref, w_ref)

    def unpack(u):
        for p in range(2):
            rows = cols[2 * u + p].astype(F32).reshape(128, 128)
            stage[pl.ds(pl.multiple_of(u * 256 + p * 128, 128), 128), :] = rows
        members = pl.ds(pl.multiple_of(u * 16, 16), 16)
        for g in range(NG):
            for r in range(4):
                rows = stage[pl.ds(u * 256 + 4 * g + r, 16, stride=16), :]
                xb[g, members, r * 128 : (r + 1) * 128] = rows.astype(BF)

    def await_state(slot):
        rcopy(
            state.at[:, pl.ds(0, 16), :], cols.at[slot], s1.at[slot], r1.at[slot], (s, sibling)
        ).wait_recv()

    loads[0].wait()
    await_state(1)
    unpack(0)

    def arrive(j):
        u = far(14 - j)
        await_state(2 * u)
        await_state(2 * u + 1)
        unpack(u)

    loop(0, 15, arrive)

    def apply(part):
        far_of = [far(4 * part + i) for i in range(4)]
        for g in range(NG):
            left = [
                w_ref[g, h, pl.ds(pl.multiple_of(u * 16, 16), 16), :] for h in range(2) for u in far_of
            ]
            both = dot(jnp.concatenate(left, 0), xb[g])
            done = both[:64] + both[64:]
            for r in range(4):
                stage2[pl.ds(4 * g + r, 64, stride=16), :] = done[:, r * 128 : (r + 1) * 128]
        for i, u in enumerate(far_of):
            for p in range(2):
                rows = stage2[pl.ds((2 * i + p) * 128, 128), :]
                outb[2 * u + p] = rows.reshape(8, 16, 128).astype(BF)
                if i == 3 and p == 0:

                    @pl.when(part < 3)
                    def _():
                        send_result(u, p).start()
                else:
                    send_result(u, p).start()

    loop(0, 4, apply)
    own_out = pltpu.make_async_copy(outb.at[0], out.at[:, rows_of(me), :], own.at[6])
    own_out.start()

    def settle(slot):
        rcopy(
            outb.at[slot], out.at[:, pl.ds(0, 16), :], s2.at[slot], r2.at[slot], (s, sibling)
        ).wait()
        rcopy(
            state.at[:, pl.ds(0, 16), :], cols.at[slot], s1.at[slot], r1.at[slot], (s, sibling)
        ).wait_send()

    loop(1, 32, settle)
    own_out.wait()

    for side in range(2):
        for k in range(4):
            hop(side, 0, k).wait_send()
            if side == 0 or k < 3:
                hop(side, 1, k).wait_send()

    def sent_wide(u):
        across(u).wait_send()
        for side in range(2):
            toward(side, lambda side=side: halo(side, u).wait_send())
            from_(side, lambda side=side: halo_across(side, u).wait_send())

    loop(0, 16, sent_wide)
    for side in range(2):
        toward(side, lambda side=side: rim(side).wait_send())


def per_device(state, obs_prior, obs_value, obs_precision, block_lists, list_counts):
    anywhere = pl.BlockSpec(memory_space=pl.ANY)
    dma = pltpu.SemaphoreType.DMA
    return pl.pallas_call(
        kernel,
        out_shape=jax.ShapeDtypeStruct(state.shape, state.dtype),
        in_specs=[pl.BlockSpec(memory_space=pltpu.HBM)] * 6,
        out_specs=anywhere,
        scratch_shapes=[
            pltpu.SMEM((NG, 16), jnp.int32),
            pltpu.SMEM((NG,), jnp.int32),
            pltpu.VMEM((3, 32, 8, 16, 128), BF),
            pltpu.VMEM((3, 2, 16, 128), F32),
            pltpu.VMEM((4096 + 16, 128), F32),
            pltpu.VMEM((48, MEM, 128), BF),
            pltpu.VMEM((48, 1, 128), F32),
            pltpu.VMEM((48, 1, 128), F32),
            pltpu.VMEM((NG, MEM, MEM), F32),
            pltpu.VMEM((NG, 16, MEM), F32),
            pltpu.VMEM((NG, 2, MEM, MEM), BF),
            pltpu.VMEM((NG, 2, MEM, MEM), BF),
            pltpu.VMEM((NG, 2, MEM, MEM), BF),
            pltpu.VMEM((32, 8, 16, 128), BF),
            pltpu.VMEM((NG, MEM, 512), BF),
            pltpu.VMEM((1024 + 16, 128), F32),
            pltpu.VMEM((32, 8, 16, 128), BF),
            dma((2, 4)), dma((2, 4)), dma((2, 4)), dma((2, 4)), dma((16,)), dma((16,)),
            dma((2, 16)), dma((2, 16)), dma((2, 16)), dma((2, 16)), dma((2,)), dma((2,)),
            dma((32,)), dma((32,)), dma((32,)), dma((32,)), dma((7,)),
        ],
        compiler_params=pltpu.CompilerParams(
            collective_id=0, has_side_effects=True, vmem_limit_bytes=62 << 20
        ),
        name="analysis",
    )(block_lists, list_counts, state, obs_prior, obs_value, obs_precision)


def solution(mesh):
    in_specs = (
        P("member", "space", None),
        P("member", "space", None),
        P("space", None),
        P("space", None),
        P(("space", "member"), None),
        P(("space", "member")),
    )
    out_specs = P("member", "space", None)
    return jax.shard_map(
        per_device, mesh=mesh, in_specs=in_specs, out_specs=out_specs, check_vma=False
    )
```
